32 devices in a mesh: groups: 2 (over x), seq: 16 (over z, y, core).
Axes of the slice: x: 2, y: 2, z: 4, core: 2. Of those that a mesh axis runs over, the one named last changes fastest.
Arguments:
- spectral: bfloat16 [8192, 4096], P(('groups', 'seq')), parts along dimension 0, may hold values from -25 to 25
- recording_lengths: int32 [8], P('groups'), parts along dimension 0, may hold values from 1 to 1024, as said below
- expert_ids: int32 [4096, 8], P(('groups', 'seq')), parts along dimension 0, may hold values from 0 to 15, all different within a row; in each aligned block of 128 rows (0 to 127, 128 to 255, ...) at most 65 rows name the same one
- gate_weights: float32 [4096, 8], P(('groups', 'seq')), parts along dimension 0, may hold values from 0.05 to 0.5
- conv_weight: bfloat16 [2304, 256], P('seq'), may hold values from -0.125 to 0.125
- conv_proj: bfloat16 [2048, 1280], P('seq'), may hold values from -0.125 to 0.125
- ln_gain: float32 [1280], replicated, may hold values from 0.25 to 1.75
- attn_in: bfloat16 [1280, 1920], P('seq'), may hold values from -8 to 8
- attn_out: bfloat16 [640, 1280], P('seq'), may hold values from -0.25 to 0.25
- audio_proj: bfloat16 [1280, 2048], P('seq'), may hold values from -0.15625 to 0.15625
- rms_gain: float32 [2048], replicated, may hold values from 0.25 to 1.75
- w_gate_up: bfloat16 [16, 2048, 1536], P('seq'), may hold values from -0.125 to 0.125
- w_down: bfloat16 [16, 768, 2048], P('seq'), may hold values from -0.21875 to 0.21875
Outputs:
- thinker_out: bfloat16 [4096, 2048], P(('groups', 'seq')), parts along dimension 0
The draws below stay inside these ranges and needn't reach their ends.
There are 2 independent parts, one for each index of `groups`. The reference program is written for one: setup_inputs(seed, part) draws one part's arguments, and reference() takes and returns one part's arrays. A program takes and returns all parts, laid end to end along the dimension named above; an argument that names none is the same for every part. Nothing has to cross between parts.
Inputs may be any that keep to these rules, and one draw needn't show every extreme that they name: `expert_ids`: each row names 8 different experts; in each aligned block of 128 rows (the rows of one device) no expert is named by more than 65 rows, a bound that some block reaches. `recording_lengths`: the lengths sum to 2048; the second recording is the longest, exactly 1024 tokens.
All inputs are finite; a program needn't handle non-finite values.
Results may differ from the reference program's by a relative error of at most 0.017.
Values may be sent and summed in bfloat16 or wider, within the bound.
No kernel may reach another device: no remote copies, remote signals or barrier semaphores. Data moves between devices by JAX's collectives and lax.ppermute only.
A program may use at most 128 MiB of HBM per device.

```python
import math
import jax
import jax.numpy as jnp
import numpy as np
from jax import lax

D = 1280
HEADS = 10
HDIM = 64
CH = 256
FI = 16
HID = 2048
FF = 768
TOPK = 8
WIN = 128
TOK_DEV = 128
TOKENS = 2048
FRAMES = 4096
FO = 8
EXPERTS = 16
SLOTS = 65
N_SEQ = 16


def draw_spectral(key, part):
    key = jax.random.fold_in(key, 11)
    first = jax.random.fold_in(key, 0)
    base = jax.random.normal(first, (FRAMES, FI * CH), jnp.float32)
    return jnp.clip(base, -6.0, 6.0).astype(jnp.bfloat16)


def draw_recording_lengths(key, part):
    key = jax.random.fold_in(key, 37)
    first_key, second_key = jax.random.split(key)
    half = TOKENS // 2
    opening = TOK_DEV // 2 + jax.random.randint(first_key, (), 0, TOKENS // 4, jnp.int32)
    remainder = half - opening
    third = 1 + jax.random.randint(second_key, (), 0, remainder - 1, jnp.int32)
    fourth = remainder - third
    return jnp.stack([opening, jnp.asarray(half, jnp.int32), third, fourth]).astype(jnp.int32)


def draw_attn_in(key, part):
    key = jax.random.fold_in(key, 23)
    first = jax.random.fold_in(key, 0)
    width = HEADS * HDIM
    base = jnp.clip(jax.random.normal(first, (D, 3 * width), jnp.float32), -5.5, 5.5) * D ** (-0.5)
    return base.astype(jnp.bfloat16)


def block_levels(key, extent, cuts, least, largest):
    def one(dim, shards_of):
        steps = jax.random.uniform(jax.random.fold_in(jax.random.fold_in(key, 6), dim), (shards_of,), jnp.float32, least / len(cuts), largest / len(cuts))
        return jnp.repeat(jnp.exp(steps), extent[dim] // shards_of).reshape((-1,) + (1,) * (len(extent) - dim - 1))

    level = one(*cuts[0])
    for cut in cuts[1:]:
        level = level * one(*cut)
    return level


def shared_out(key, own, number, rows, amount, top, most, slope):
    ranking = jax.random.permutation(key, amount)
    heavy_load, ordinary = portions_of(amount, rows * top, most, slope, True), portions_of(amount, rows * top, most, slope, False)
    places = jnp.arange(amount)

    def named(tallies, turn):
        used = int((tallies > 0).sum())
        fixed = max(1, used // 4)
        moved = fixed + (places - fixed + turn * (used - fixed)) % max(1, amount - fixed)
        return jnp.zeros((amount,), jnp.int32).at[ranking[jnp.where(places < fixed, places, moved)]].set(jnp.asarray(tallies, jnp.int32))

    tallies = jnp.where(number % 4 == 0, named(heavy_load, number // 4), named(ordinary, number - number // 4 - 1))
    mixed = jax.random.permutation(jax.random.fold_in(own, 3), amount)
    giver, sink = mixed[0:amount // 2 * 2:2], mixed[1:amount // 2 * 2:2]
    margin = jnp.minimum(tallies[giver] - 1, most - tallies[sink]) // 2
    margin = jnp.where((giver == ranking[0]) | (sink == ranking[0]) | (tallies[sink] == 0), 0, jnp.maximum(margin, 0))
    moved = jax.random.randint(jax.random.fold_in(own, 4), (amount // 2,), 0, 1 << 20) % (margin + 1)
    tallies = tallies.at[giver].add(-moved).at[sink].add(moved)
    members = jnp.searchsorted(jnp.cumsum(tallies), jnp.arange(rows * top), side="right").astype(jnp.int32)
    table = members.reshape(top, rows).T
    table = table[jax.random.permutation(jax.random.fold_in(own, 1), rows)]
    turn = jax.random.randint(jax.random.fold_in(own, 2), (rows, 1), 0, top)
    return jnp.take_along_axis(table, (jnp.arange(top)[None, :] + turn) % top, axis=1)


def portions_of(amount, total, limit, lean, full):
    portions = [(1 << 20) // math.isqrt(standing ** lean) + 1 for standing in range(1, amount + 1)]
    largest = limit if full else min(limit, max(-(-total // amount), total * portions[0] // sum(portions)))
    least = 1 if total - largest >= amount - 1 else 0
    counts, surplus = [largest] + [least] * (amount - 1), total - largest - least * (amount - 1)
    while surplus > 0:
        free = [i for i in range(1, amount) if counts[i] < largest] or [i for i in range(1, amount) if counts[i] < limit]
        whole, remaining = sum([portions[i] for i in free]), surplus
        for i in free:
            extra = min(limit - counts[i], max(1, remaining * portions[i] // whole), surplus)
            counts[i] = counts[i] + extra
            surplus = surplus - extra
    return np.array(counts)


def gaussian(rng, extent, scale, most, shards=(), held_as=jnp.bfloat16):
    factor_of = block_levels(rng, extent, shards, -0.22, 0.18) if shards else 1.0
    entries = jax.random.normal(rng, extent, jnp.float32) * scale * factor_of
    return jnp.minimum(jnp.maximum(entries, -most), most).astype(held_as)


def setup_inputs(seed: int = 0, part: int = 0) -> dict:
    streams_of = jax.random.split(jax.random.key(seed), 14)
    part_splits = jax.random.split(jax.random.fold_in(streams_of[13], part), 14)
    spectral = draw_spectral(jax.random.fold_in(jax.random.fold_in(streams_of[13], part), 71), part)
    recording_lengths = draw_recording_lengths(jax.random.fold_in(jax.random.fold_in(streams_of[13], part), 71), part)
    expert_ids_keys = jax.random.split(jax.random.fold_in(part_splits[2], 1), TOKENS // TOK_DEV)
    expert_ids_turns = jax.random.permutation(jax.random.fold_in(part_splits[2], 3), TOKENS // TOK_DEV)
    expert_ids = jax.vmap(lambda own, number: shared_out(jax.random.fold_in(part_splits[2], 2), own, number, TOK_DEV, EXPERTS, TOPK, SLOTS, 2))(expert_ids_keys, expert_ids_turns).reshape((TOKENS, TOPK))
    gate_weights = jnp.clip(jnp.exp(math.log(0.5) - 2.3025851 * jax.random.uniform(part_splits[3], (TOKENS, TOPK), jnp.float32) ** block_levels(part_splits[3], (TOKENS, TOPK), ((0, 16),), -0.2, 0.2)), 0.05, 0.5)
    conv_weight = gaussian(streams_of[4], (9 * CH, CH), (9 * CH) ** -0.5, 0.125, ((0, 16),))
    conv_proj = gaussian(streams_of[5], (FO * CH, D), (FO * CH) ** -0.5, 0.125, ((0, 16),))
    ln_gain = jnp.clip(1.0 + 0.15 * jax.random.normal(streams_of[6], (D,), jnp.float32), 0.25, 1.75)
    attn_in = draw_attn_in(jax.random.fold_in(streams_of[13], 71), part)
    attn_out = gaussian(streams_of[8], (HEADS * HDIM, D), (HEADS * HDIM) ** -0.5, 0.25, ((0, 16),))
    audio_proj = gaussian(streams_of[9], (D, HID), D ** -0.5, 0.15625, ((0, 16),))
    rms_gain = jnp.clip(1.0 + 0.15 * jax.random.normal(streams_of[10], (HID,), jnp.float32), 0.25, 1.75)
    w_gate_up = gaussian(streams_of[11], (EXPERTS, HID, 2 * FF), HID ** -0.5, 0.125, ((0, 16),))
    w_down = gaussian(streams_of[12], (EXPERTS, FF, HID), FF ** -0.5, 0.21875, ((0, 16),))
    return {"spectral": spectral, "recording_lengths": recording_lengths, "expert_ids": expert_ids, "gate_weights": gate_weights, "conv_weight": conv_weight, "conv_proj": conv_proj, "ln_gain": ln_gain, "attn_in": attn_in, "attn_out": attn_out, "audio_proj": audio_proj, "rms_gain": rms_gain, "w_gate_up": w_gate_up, "w_down": w_down}


def layer_norm(values):
    mean = lax.optimization_barrier(jnp.mean(values, -1, keepdims=True))
    centered = values - mean
    variance = lax.optimization_barrier(jnp.mean(centered * centered, -1, keepdims=True))
    return centered * lax.rsqrt(variance + 1e-05)

def rms_norm(values, gain):
    scaled = values.astype(jnp.float32)
    power = lax.optimization_barrier(jnp.mean(scaled * scaled, -1, keepdims=True))
    return (scaled * lax.rsqrt(power + 1e-06) * gain).astype(jnp.bfloat16)

def recording_of(positions, ends):
    return lax.optimization_barrier(jnp.sum((positions[:, None] >= ends[None, :]).astype(jnp.int32), 1))

def attend(query_rows, key_rows, query_pos, key_pos, ends, total):
    width = HEADS * HDIM
    count = query_rows.shape[0]
    keys_count = key_rows.shape[0]
    query = query_rows.reshape(count, HEADS, HDIM).astype(jnp.float32)
    keys = key_rows[:, :width].reshape(keys_count, HEADS, HDIM).astype(jnp.float32)
    values = key_rows[:, width:].reshape(keys_count, HEADS, HDIM).astype(jnp.float32)
    scores = jnp.einsum('qhd,khd->hqk', query, keys) * HDIM ** (-0.5)
    same = recording_of(query_pos, ends)[:, None] == recording_of(key_pos, ends)[None, :]
    near = jnp.abs(query_pos[:, None] - key_pos[None, :]) <= WIN
    inside = (key_pos >= 0) & (key_pos < total)
    valid = same & near & inside[None, :]
    scores = jnp.where(valid[None], scores, -1e+30)
    top = lax.optimization_barrier(jnp.max(scores, -1, keepdims=True))
    weights = jnp.exp(scores - top)
    probs = (weights / lax.optimization_barrier(jnp.sum(weights, -1, keepdims=True))).astype(jnp.bfloat16)
    context = jnp.einsum('hqk,khd->qhd', probs.astype(jnp.float32), values)
    return context.reshape(count, width).astype(jnp.bfloat16)

def expert_ffn(rows, gate_up, down):
    both = jnp.dot(rows, gate_up, preferred_element_type=jnp.float32)
    inner = down.shape[0]
    hidden = (jax.nn.silu(both[:, :inner]) * both[:, inner:]).astype(jnp.bfloat16)
    return jnp.dot(hidden, down, preferred_element_type=jnp.float32).astype(jnp.bfloat16)

def reference(spectral, recording_lengths, expert_ids, gate_weights, conv_weight, conv_proj, ln_gain, attn_in, attn_out, audio_proj, rms_gain, w_gate_up, w_down):
    width = HEADS * HDIM
    grid = spectral.reshape(FRAMES, FI, CH)
    padded = jnp.pad(grid, ((1, 0), (1, 0), (0, 0)))
    conv_sum = jnp.zeros((TOKENS * FO, CH), jnp.float32)
    for across in range(3):
        row_set = padded[across:across + 2 * TOKENS:2]
        for along in range(3):
            tap_rows = row_set[:, along:along + FI:2, :].reshape(TOKENS * FO, CH)
            index = 3 * across + along
            kernel = conv_weight[index * CH:(index + 1) * CH]
            conv_sum = conv_sum + jnp.dot(tap_rows, kernel, preferred_element_type=jnp.float32)
    conv_act = jax.nn.gelu(conv_sum, approximate=False).astype(jnp.bfloat16).reshape(TOKENS, FO * CH)
    embed = jnp.dot(conv_act, conv_proj, preferred_element_type=jnp.float32).astype(jnp.bfloat16)
    normed = (layer_norm(embed.astype(jnp.float32)) * ln_gain).astype(jnp.bfloat16)
    qkv = jnp.dot(normed, attn_in, preferred_element_type=jnp.float32).astype(jnp.bfloat16)
    ends = jnp.cumsum(recording_lengths).astype(jnp.int32)
    key_pad = jnp.pad(qkv[:, width:], ((WIN, WIN), (0, 0)))

    def block(number):
        first = (number * TOK_DEV).astype(jnp.int32)
        query_rows = lax.dynamic_slice_in_dim(qkv[:, :width], first, TOK_DEV, 0)
        key_rows = lax.dynamic_slice_in_dim(key_pad, first, TOK_DEV + 2 * WIN, 0)
        query_pos = first + jnp.arange(TOK_DEV, dtype=jnp.int32)
        key_pos = first - WIN + jnp.arange(TOK_DEV + 2 * WIN, dtype=jnp.int32)
        return attend(query_rows, key_rows, query_pos, key_pos, ends, TOKENS)
    context = lax.map(block, jnp.arange(N_SEQ, dtype=jnp.int32)).reshape(TOKENS, width)
    mixed = embed.astype(jnp.float32) + jnp.dot(context, attn_out, preferred_element_type=jnp.float32)
    encoded = mixed.astype(jnp.bfloat16)
    post = layer_norm(encoded.astype(jnp.float32)).astype(jnp.bfloat16)
    audio_embed = jnp.dot(post, audio_proj, preferred_element_type=jnp.float32).astype(jnp.bfloat16)
    thinker_in = rms_norm(audio_embed, rms_gain)
    grouped = expert_ids.reshape(N_SEQ, TOK_DEV * TOPK)
    onehot = (grouped[:, :, None] == jnp.arange(EXPERTS, dtype=jnp.int32)[None, None, :]).astype(jnp.int32)
    before = jnp.cumsum(onehot, 1) - onehot
    position = lax.optimization_barrier(jnp.sum(before * onehot, 2))
    source = jnp.arange(N_SEQ, dtype=jnp.int32)[:, None]
    flat_slot = (grouped * (N_SEQ * SLOTS) + source * SLOTS + position).reshape(TOKENS, TOPK)
    owner = jnp.full((EXPERTS * N_SEQ * SLOTS,), TOKENS * TOPK, jnp.int32)
    owner = owner.at[flat_slot.reshape(-1)].set(jnp.arange(TOKENS * TOPK, dtype=jnp.int32))
    owner_rows = (owner // TOPK).reshape(EXPERTS, N_SEQ * SLOTS)
    padded_rows = jnp.concatenate([thinker_in, jnp.zeros((1, HID), jnp.bfloat16)], 0)

    def one_expert(number):
        rows = padded_rows[owner_rows[number]]
        return expert_ffn(rows, w_gate_up[number], w_down[number])
    results = lax.map(one_expert, jnp.arange(EXPERTS, dtype=jnp.int32)).reshape(EXPERTS * N_SEQ * SLOTS, HID)
    total = audio_embed.astype(jnp.float32)
    for choice_k in range(TOPK):
        picked = results[flat_slot[:, choice_k]]
        total = total + gate_weights[:, choice_k:choice_k + 1] * picked
    return total.astype(jnp.bfloat16)
```

```python
import jax
import jax.numpy as jnp
from jax import lax
from jax.sharding import PartitionSpec as P

HEADS = 10
HDIM = 64
WIN = 128


def shifted(block, axis, distance):
    devices = range(lax.axis_size(axis))
    route = [(i - distance, i) for i in devices if i - distance in devices]
    return lax.ppermute(block, axis, route)


def padded(cells, sides, width):
    for axis, dim in sides:
        count = lax.axis_size(axis)
        ends = count - 1
        head = lax.slice_in_dim(cells, 0, width, axis=dim)
        tail = lax.slice_in_dim(cells, cells.shape[dim] - width, cells.shape[dim], axis=dim)
        cells = jnp.concatenate(
            [
                lax.ppermute(tail, axis, [(i, (i + 1) % count) for i in range(ends)]),
                cells,
                lax.ppermute(head, axis, [((i + 1) % count, i) for i in range(ends)]),
            ],
            axis=dim,
        )
    return cells


def layer_norm(values):
    mean = jnp.mean(values, -1, keepdims=True)
    centered = values - mean
    variance = jnp.mean(centered * centered, -1, keepdims=True)
    return centered * lax.rsqrt(variance + 1e-05)


def rms_norm(values, gain):
    scaled = values.astype(jnp.float32)
    power = jnp.mean(scaled * scaled, -1, keepdims=True)
    return (scaled * lax.rsqrt(power + 1e-06) * gain).astype(jnp.bfloat16)


def recording_of(positions, ends):
    return jnp.sum((positions[:, None] >= ends[None, :]).astype(jnp.int32), 1)


def attend(query_rows, key_rows, query_pos, key_pos, ends, total):
    width = HEADS * HDIM
    count = query_rows.shape[0]
    keys_count = key_rows.shape[0]
    query = query_rows.reshape(count, HEADS, HDIM)
    keys = key_rows[:, :width].reshape(keys_count, HEADS, HDIM)
    values = key_rows[:, width:].reshape(keys_count, HEADS, HDIM)
    scores = jnp.einsum("qhd,khd->hqk", query, keys, preferred_element_type=jnp.float32) * HDIM ** (
        -0.5
    )
    same = recording_of(query_pos, ends)[:, None] == recording_of(key_pos, ends)[None, :]
    near = jnp.abs(query_pos[:, None] - key_pos[None, :]) <= WIN
    inside = (key_pos >= 0) & (key_pos < total)
    valid = same & near & inside[None, :]
    scores = jnp.where(valid[None], scores, -1e30)
    top = jnp.max(scores, -1, keepdims=True)
    weights = jnp.exp(scores - top)
    probs = (weights / jnp.sum(weights, -1, keepdims=True)).astype(jnp.bfloat16)
    context = jnp.einsum("hqk,khd->qhd", probs, values, preferred_element_type=jnp.float32)
    return context.reshape(count, width).astype(jnp.bfloat16)


def expert_ffn(rows, gate_up, down):
    both = jnp.dot(rows, gate_up, preferred_element_type=jnp.float32)
    inner = down.shape[0]
    hidden = (jax.nn.silu(both[:, :inner]) * both[:, inner:]).astype(jnp.bfloat16)
    return jnp.dot(hidden, down, preferred_element_type=jnp.float32).astype(jnp.bfloat16)


def fold_with(left, piece):
    return jnp.dot(left, piece, preferred_element_type=jnp.float32)


def ring_step(block, stride, size):
    route = []
    for i in range(lax.axis_size("seq")):
        place = i // stride % size
        route.append((i, i + ((place + 1) % size - place) * stride))
    return lax.ppermute(block, "seq", route)


def levels(devices):
    core = 2
    rest = devices // core
    y = 1
    while (2 * y) * (2 * y) <= rest:
        y *= 2
    return rest // y, y, core


def gate_table(expert_ids, gate_weights, experts):
    named = expert_ids[None] == jnp.arange(experts, dtype=jnp.int32)[:, None, None]
    return jnp.sum(jnp.where(named, gate_weights[None], 0.0), -1)


def dense_experts(audio_embed, scaled, gates, fused, down):
    devices = lax.axis_size("seq")
    zs, ys, cores = levels(devices)
    tokens = scaled.shape[0]
    me = lax.axis_index("seq")
    z, y, core = me // (ys * cores), me // cores % ys, me % cores
    table = lax.dynamic_index_in_dim(gates, me, 1, keepdims=False)
    inner = down.shape[0]
    width = down.shape[1]
    blocks = [scaled]
    for _ in range(zs - 1):
        blocks.append(ring_step(blocks[-1], ys * cores, zs))
    chunks = []
    for block in blocks:
        line = [block]
        for _ in range(ys - 1):
            line.append(ring_step(line[-1], cores, ys))
        pair = jnp.stack(line)
        chunks.append(jnp.stack([pair, ring_step(pair, 1, cores)]))
    carry = None
    for k in list(range(1, zs)) + [0]:
        rows = chunks[k].reshape(-1, scaled.shape[1])
        source = (z - k) % zs * (ys * cores)
        weights = []
        for dc in range(cores):
            for dy in range(ys):
                index = source + (y - dy) % ys * cores + (core - dc) % cores
                weights.append(lax.dynamic_index_in_dim(table, index, 0, keepdims=False))
        weight = jnp.concatenate(weights)[:, None]
        both = jnp.dot(rows, fused, preferred_element_type=jnp.float32)
        hidden = (jax.nn.silu(both[:, :inner]) * both[:, inner:] * weight).astype(jnp.bfloat16)
        sums = jnp.dot(hidden, down, preferred_element_type=jnp.float32)
        sums = sums.reshape(cores, ys, tokens, width)
        theirs = ring_step(sums[1].astype(jnp.bfloat16), 1, cores)
        chip = sums[0] + theirs.astype(jnp.float32)
        if ys > 1:
            acc = chip[1].astype(jnp.bfloat16)
            for dy in range(1, ys):
                moved = ring_step(acc, cores, ys).astype(jnp.float32)
                mine = chip[(dy + 1) % ys]
                acc = moved + mine
                if dy < ys - 1:
                    acc = acc.astype(jnp.bfloat16)
            column = acc
        else:
            column = chip[0]
        if carry is not None:
            column = column + carry.astype(jnp.float32)
        if k:
            carry = ring_step(column.astype(jnp.bfloat16), ys * cores, zs)
    return (audio_embed.astype(jnp.float32) + column).astype(jnp.bfloat16)


def on_device(
    spectral,
    recording_lengths,
    expert_ids,
    gate_weights,
    conv_weight,
    conv_proj,
    ln_gain,
    attn_in,
    attn_out,
    audio_proj,
    rms_gain,
    w_gate_up,
    w_down,
):
    devices = lax.axis_size("seq")
    local_tokens = expert_ids.shape[0]
    topk = expert_ids.shape[1]
    experts = devices * w_down.shape[0]
    slots = local_tokens * topk // experts + 1
    width = HEADS * HDIM
    channels = conv_weight.shape[1]
    freq_in = spectral.shape[1] // channels
    freq_out = freq_in // 2
    thinker_width = audio_proj.shape[1]
    proj_full = lax.all_gather(audio_proj, "seq", axis=0, tiled=True)
    frame_rim = shifted(spectral[-1:], "seq", 1)
    extended = jnp.concatenate([frame_rim, spectral], 0).reshape(
        2 * local_tokens + 1, freq_in, channels
    )
    extended = jnp.pad(extended, ((0, 0), (1, 0), (0, 0)))
    tap_list = []
    for across in range(3):
        row_set = extended[across : across + 2 * local_tokens : 2]
        for along in range(3):
            tap_list.append(row_set[:, along : along + freq_in : 2, :])
    patches = jnp.concatenate(tap_list, 2).reshape(local_tokens * freq_out, 9 * channels)
    conv_sum = fold_with(patches, lax.all_gather(conv_weight, "seq", axis=0, tiled=True))
    conv_act = (
        jax.nn.gelu(conv_sum, approximate=False)
        .astype(jnp.bfloat16)
        .reshape(local_tokens, freq_out * channels)
    )
    embed_sum = fold_with(conv_act, lax.all_gather(conv_proj, "seq", axis=0, tiled=True))
    embed = embed_sum.astype(jnp.bfloat16)
    normed = (layer_norm(embed.astype(jnp.float32)) * ln_gain).astype(jnp.bfloat16)
    qkv_sum = fold_with(normed, lax.all_gather(attn_in, "seq", axis=0, tiled=True))
    qkv = qkv_sum.astype(jnp.bfloat16)
    key_rows = padded(qkv[:, width:], (("seq", 0),), WIN)
    ends = jnp.cumsum(recording_lengths)
    first = lax.axis_index("seq") * local_tokens
    query_pos = first + jnp.arange(local_tokens, dtype=jnp.int32)
    key_pos = first - WIN + jnp.arange(local_tokens + 2 * WIN, dtype=jnp.int32)
    context = attend(qkv[:, :width], key_rows, query_pos, key_pos, ends, devices * local_tokens)
    branch_sum = fold_with(context, lax.all_gather(attn_out, "seq", axis=0, tiled=True))
    encoded = (embed.astype(jnp.float32) + branch_sum).astype(jnp.bfloat16)
    post = layer_norm(encoded.astype(jnp.float32)).astype(jnp.bfloat16)
    audio_embed = jnp.dot(post, proj_full, preferred_element_type=jnp.float32).astype(jnp.bfloat16)
    if experts <= 2 * topk and devices % 2 == 0:
        power = jnp.mean(jnp.square(audio_embed.astype(jnp.float32)), -1, keepdims=True)
        scaled = (post.astype(jnp.float32) * lax.rsqrt(power + 1e-06)).astype(jnp.bfloat16)
        gates = lax.all_gather(gate_table(expert_ids, gate_weights, experts), "seq", axis=0)
        weighted = (w_gate_up[0] * rms_gain[:, None]).astype(jnp.bfloat16)
        fused = jnp.dot(proj_full, weighted, preferred_element_type=jnp.float32)
        return dense_experts(audio_embed, scaled, gates, fused.astype(jnp.bfloat16), w_down[0])
    flat_ids = expert_ids.reshape(-1)
    onehot = (flat_ids[:, None] == jnp.arange(experts, dtype=jnp.int32)[None, :]).astype(jnp.int32)
    before = jnp.cumsum(onehot, 0) - onehot
    position = jnp.sum(before * onehot, 1)
    slot_index = flat_ids * slots + position
    owner = jnp.full((experts * slots,), local_tokens * topk, jnp.int32)
    owner = owner.at[slot_index].set(jnp.arange(local_tokens * topk, dtype=jnp.int32))
    owner_rows = owner // topk
    gate_up_local = w_gate_up[0]
    down_local = w_down[0]
    sent_rows = rms_norm(audio_embed, rms_gain)
    padded_rows = jnp.concatenate([sent_rows, jnp.zeros((1, sent_rows.shape[1]), jnp.bfloat16)], 0)
    send_buffer = padded_rows[owner_rows].reshape(experts, slots, sent_rows.shape[1])
    received = lax.all_to_all(send_buffer, "seq", split_axis=0, concat_axis=0, tiled=True)
    rows = received.reshape(-1, received.shape[-1])
    result = expert_ffn(rows, gate_up_local, down_local)
    results = result.reshape(received.shape[0], received.shape[1], thinker_width)
    returned = lax.all_to_all(results, "seq", split_axis=0, concat_axis=0, tiled=True)
    picked = returned.reshape(experts * slots, thinker_width)[slot_index].reshape(
        local_tokens, topk, thinker_width
    )
    expert_sum = jnp.sum(picked * gate_weights[:, :, None], 1)
    return (audio_embed.astype(jnp.float32) + expert_sum).astype(jnp.bfloat16)


def solution(mesh):
    placed = (
        P(("groups", "seq"), None),
        P("groups"),
        P(("groups", "seq"), None),
        P(("groups", "seq"), None),
        P("seq", None),
        P("seq", None),
        P(),
        P("seq", None),
        P("seq", None),
        P("seq", None),
        P(),
        P("seq", None, None),
        P("seq", None, None),
    )
    return jax.shard_map(
        on_device, mesh=mesh, in_specs=placed, out_specs=P(("groups", "seq"), None), check_vma=False
    )
```

```python
import functools

import jax
import jax.numpy as jnp
from jax import lax
from jax.experimental import pallas as pl
from jax.experimental.pallas import tpu as pltpu
from jax.sharding import PartitionSpec as P

HEADS = 10
HDIM = 64
WIN = 128


def shifted(block, axis, distance):
    devices = range(lax.axis_size(axis))
    route = [(i - distance, i) for i in devices if i - distance in devices]
    return lax.ppermute(block, axis, route)


def padded(cells, sides, width):
    for axis, dim in sides:
        count = lax.axis_size(axis)
        ends = count - 1
        head = lax.slice_in_dim(cells, 0, width, axis=dim)
        tail = lax.slice_in_dim(cells, cells.shape[dim] - width, cells.shape[dim], axis=dim)
        cells = jnp.concatenate(
            [
                lax.ppermute(tail, axis, [(i, (i + 1) % count) for i in range(ends)]),
                cells,
                lax.ppermute(head, axis, [((i + 1) % count, i) for i in range(ends)]),
            ],
            axis=dim,
        )
    return cells


def layer_norm(values):
    mean = jnp.mean(values, -1, keepdims=True)
    centered = values - mean
    variance = jnp.mean(centered * centered, -1, keepdims=True)
    return centered * lax.rsqrt(variance + 1e-05)


def rms_norm(values, gain):
    scaled = values.astype(jnp.float32)
    power = jnp.mean(scaled * scaled, -1, keepdims=True)
    return (scaled * lax.rsqrt(power + 1e-06) * gain).astype(jnp.bfloat16)


def recording_of(positions, ends):
    return jnp.sum((positions[:, None] >= ends[None, :]).astype(jnp.int32), 1)


def attend(query_rows, key_rows, query_pos, key_pos, ends, total):
    width = HEADS * HDIM
    count = query_rows.shape[0]
    keys_count = key_rows.shape[0]
    query = query_rows.reshape(count, HEADS, HDIM)
    keys = key_rows[:, :width].reshape(keys_count, HEADS, HDIM)
    values = key_rows[:, width:].reshape(keys_count, HEADS, HDIM)
    scores = jnp.einsum("qhd,khd->hqk", query, keys, preferred_element_type=jnp.float32) * HDIM ** (
        -0.5
    )
    same = recording_of(query_pos, ends)[:, None] == recording_of(key_pos, ends)[None, :]
    near = jnp.abs(query_pos[:, None] - key_pos[None, :]) <= WIN
    inside = (key_pos >= 0) & (key_pos < total)
    valid = same & near & inside[None, :]
    scores = jnp.where(valid[None], scores, -1e30)
    top = jnp.max(scores, -1, keepdims=True)
    weights = jnp.exp(scores - top)
    probs = (weights / jnp.sum(weights, -1, keepdims=True)).astype(jnp.bfloat16)
    context = jnp.einsum("hqk,khd->qhd", probs, values, preferred_element_type=jnp.float32)
    return context.reshape(count, width).astype(jnp.bfloat16)


def expert_ffn(rows, gate_up, down):
    both = jnp.dot(rows, gate_up, preferred_element_type=jnp.float32)
    inner = down.shape[0]
    hidden = (jax.nn.silu(both[:, :inner]) * both[:, inner:]).astype(jnp.bfloat16)
    return jnp.dot(hidden, down, preferred_element_type=jnp.float32).astype(jnp.bfloat16)


def fold_with(left, piece):
    return jnp.dot(left, piece, preferred_element_type=jnp.float32)


def ring_step(block, stride, size):
    route = []
    for i in range(lax.axis_size("seq")):
        place = i // stride % size
        route.append((i, i + ((place + 1) % size - place) * stride))
    return lax.ppermute(block, "seq", route)


def levels(devices):
    core = 2
    rest = devices // core
    y = 1
    while (2 * y) * (2 * y) <= rest:
        y *= 2
    return rest // y, y, core


def gate_table(expert_ids, gate_weights, experts):
    named = expert_ids[None] == jnp.arange(experts, dtype=jnp.int32)[:, None, None]
    return jnp.sum(jnp.where(named, gate_weights[None], 0.0), -1)


def spread_gates(table):
    zs, ys, cores = levels(lax.axis_size("seq"))
    blocks = [table]
    for _ in range(zs - 1):
        blocks.append(ring_step(blocks[-1], ys * cores, zs))
    line = [jnp.stack(blocks)]
    for _ in range(ys - 1):
        line.append(ring_step(line[-1], cores, ys))
    both = jnp.stack(line)
    both = jnp.stack([both, ring_step(both, 1, cores)])
    mine = lax.dynamic_index_in_dim(both, lax.axis_index("seq"), 3, keepdims=False)
    return [mine[:, :, k].reshape(-1) for k in range(zs)]


def dense_experts(audio_embed, scaled, gates, fused, down):
    devices = lax.axis_size("seq")
    zs, ys, cores = levels(devices)
    tokens = scaled.shape[0]
    inner = down.shape[0]
    width = down.shape[1]
    blocks = [scaled]
    for _ in range(zs - 1):
        blocks.append(ring_step(blocks[-1], ys * cores, zs))
    chunks = []
    for block in blocks:
        line = [block]
        for _ in range(ys - 1):
            line.append(ring_step(line[-1], cores, ys))
        pair = jnp.stack(line)
        chunks.append(jnp.stack([pair, ring_step(pair, 1, cores)]))
    carry = None
    crossed = []
    columns = {}
    for k in list(range(1, zs)) + [0]:
        rows = chunks[k].reshape(-1, scaled.shape[1])
        weight = gates[k][:, None]
        both = jnp.dot(rows, fused, preferred_element_type=jnp.float32)
        hidden = (jax.nn.silu(both[:, :inner]) * both[:, inner:] * weight).astype(jnp.bfloat16)
        sums = jnp.dot(hidden, down, preferred_element_type=jnp.float32).astype(jnp.bfloat16)
        sums = sums.reshape(cores, ys, tokens, width)
        theirs = ring_step(sums[1], 1, cores)
        crossed.append(theirs)
        chip = sums[0].astype(jnp.float32) + theirs.astype(jnp.float32)
        column = chip[1 % ys]
        for dy in range(1, ys):
            moved = ring_step(column.astype(jnp.bfloat16), cores, ys)
            column = moved.astype(jnp.float32) + chip[(dy + 1) % ys]
        columns[k] = column
    for k in list(range(1, zs)) + [0]:
        column = columns[k]
        if carry is not None:
            column = column + carry.astype(jnp.float32)
        if k:
            carry = ring_step(column.astype(jnp.bfloat16), ys * cores, zs)
    return (audio_embed.astype(jnp.float32) + column).astype(jnp.bfloat16)


def hop(block, stride, size, distance):
    route = []
    for i in range(lax.axis_size("seq")):
        place = i // stride % size
        route.append((i, i + ((place + distance) % size - place) * stride))
    return lax.ppermute(block, "seq", route)


def after(block, *others):
    return lax.optimization_barrier((block, *others))[0]


def spread(block, halves=1, late=None):
    zs, ys, cores = levels(lax.axis_size("seq"))
    if halves > 1:
        rows = block.shape[0] // halves
        block = lax.dynamic_slice_in_dim(block, lax.axis_index("groups") * rows, rows, 0)
    far = [hop(block, ys * cores, zs, k) for k in range(1, zs)]
    side = [hop(block, cores, ys, j) for j in range(1, ys)]
    stacks = [jnp.stack([block, *side, *far])]
    names = [[(0, j, 0, 0) for j in range(ys)] + [(k, 0, 0, 0) for k in range(1, zs)]]
    for j in range(1, ys):
        stacks.append(hop(stacks[0][ys:], cores, ys, j))
        names.append([(k, j, 0, 0) for k in range(1, zs)])
    if halves > 1:
        for i in range(len(stacks)):
            stacks.append(lax.ppermute(stacks[i], "groups", [(0, 1), (1, 0)]))
            names.append([(k, j, 0, 1) for k, j, _, _ in names[i]])
    for i in range(len(stacks)):
        sent = stacks[i] if late is None else after(stacks[i], late())
        stacks.append(hop(sent, 1, cores, 1))
        names.append([(k, j, 1, dx) for k, j, _, dx in names[i]])
    return stacks, names


def put_in_place(names, place, pieces, full, sems):
    halves = 1 + max(name[3] for stack in names for name in stack)
    rows = pieces[0].shape[1]
    zs, ys, cores = levels(full.shape[0] // (halves * rows))
    z, y, core, group = place[0], place[1], place[2], place[3]
    copies = []
    for piece, stack in zip(pieces, names):
        for i, (k, dy, dc, dx) in enumerate(stack):
            index = lax.rem(z - k + zs, zs) * ys + lax.rem(y - dy + ys, ys)
            index = index * cores + lax.rem(core - dc + cores, cores)
            start = index * (rows * halves)
            if halves > 1:
                start = start + lax.rem(group - dx + halves, halves) * rows
            copies.append(
                pltpu.make_async_copy(
                    piece.at[i],
                    full.at[pl.ds(pl.multiple_of(start, rows), rows)],
                    sems.at[len(copies)],
                )
            )
    for copy in copies:
        copy.start()
    for copy in copies:
        copy.wait()


def norm_rows(values):
    mean = jnp.mean(values, -1, keepdims=True)
    centered = values - mean
    variance = jnp.mean(centered * centered, -1, keepdims=True)
    return centered * lax.rsqrt(variance + 1e-05)


def conv_kernel(names, place, frames, rim, *refs):
    pieces, (out, taps, weight, sems) = refs[: len(names)], refs[-4:]
    tokens = out.shape[0]
    channels = weight.shape[1]
    bins = out.shape[1] // channels
    row = lax.broadcasted_iota(jnp.int32, (tokens, 2 * tokens), 0)
    column = lax.broadcasted_iota(jnp.int32, (tokens, 2 * tokens), 1)
    first = lax.broadcasted_iota(jnp.int32, (tokens, 2 * channels), 0) == 0
    for a in range(3):
        pick = jnp.where(column == 2 * row + a - 1, 1.0, 0.0).astype(jnp.bfloat16)
        taps[a, :tokens, :] = jnp.zeros((tokens, 2 * channels), jnp.bfloat16)
        for f in range(bins):
            span = slice(2 * f * channels, 2 * (f + 1) * channels)
            part = jnp.dot(pick, frames[:, span], preferred_element_type=jnp.float32)
            if a == 0:
                part = jnp.where(first, rim[:, span].astype(jnp.float32), part)
            taps[a, (f + 1) * tokens : (f + 2) * tokens, :] = part.astype(jnp.bfloat16)
    put_in_place(names, place, pieces, weight, sems)
    half = bins // 2 * tokens
    for part in range(2):
        total = jnp.zeros((half, channels), jnp.float32)
        low = part * half
        for a in range(3):
            base = 3 * a * channels
            total += jnp.dot(
                taps[a, low + tokens : low + tokens + half, :],
                weight[base + channels : base + 3 * channels],
                preferred_element_type=jnp.float32,
            )
            total += jnp.dot(
                taps[a, low : low + half, channels:],
                weight[base : base + channels],
                preferred_element_type=jnp.float32,
            )
        act = (0.5 * total * (1.0 + lax.erf(total * 0.7071067811865476))).astype(jnp.bfloat16)
        for f in range(bins // 2):
            where = (part * (bins // 2) + f) * channels
            out[:, where : where + channels] = act[f * tokens : (f + 1) * tokens]


def fetch(gathered, rows, first, full, sems):
    copies = [
        pltpu.make_async_copy(
            gathered.at[i, :rows, first : first + full.shape[1]],
            full.at[i * rows : (i + 1) * rows],
            sems.at[i],
        )
        for i in range(gathered.shape[0])
    ]
    for copy in copies:
        copy.start()
    for copy in copies:
        copy.wait()


def embed_kernel(rows, act, gain, gathered, embed, normed, weight, sems):
    fetch(gathered, rows, 0, weight, sems)
    step = 256
    for low in range(0, embed.shape[1], step):
        span = slice(low, low + step)
        sums = jnp.dot(act[...], weight[:, span], preferred_element_type=jnp.float32)
        embed[:, span] = sums.astype(jnp.bfloat16)
    kept = embed[...].astype(jnp.float32)
    normed[...] = (norm_rows(kept) * gain[...]).astype(jnp.bfloat16)


def qkv_kernel(first, normed, gathered, query, key_rows, weight, sems):
    fetch(gathered, weight.shape[0] // gathered.shape[0], first, weight, sems)
    width = query.shape[1]
    query[...] = jnp.dot(
        normed[...], weight[:, :width], preferred_element_type=jnp.float32
    ).astype(jnp.bfloat16)
    key_rows[...] = jnp.dot(
        normed[...], weight[:, width:], preferred_element_type=jnp.float32
    ).astype(jnp.bfloat16)


def attend_kernel(total, ends, first, query, left, own, right, embed, out_proj, *refs):
    encoded, post, ctx = refs[-3:]
    tokens, width = query.shape
    reach = left.shape[0]
    keys = tokens + 2 * reach
    query_pos = first[0] + lax.broadcasted_iota(jnp.int32, (tokens, keys), 0)
    key_pos = first[0] - reach + lax.broadcasted_iota(jnp.int32, (tokens, keys), 1)
    query_rec = jnp.zeros((tokens, keys), jnp.int32)
    key_rec = jnp.zeros((tokens, keys), jnp.int32)
    for r in range(ends.shape[0]):
        query_rec += (query_pos >= ends[r]).astype(jnp.int32)
        key_rec += (key_pos >= ends[r]).astype(jnp.int32)
    near = jnp.abs(query_pos - key_pos) <= WIN
    valid = (query_rec == key_rec) & near & (key_pos >= 0) & (key_pos < total)
    low = lax.broadcasted_iota(jnp.int32, (tokens, 2 * HDIM), 1) < HDIM
    sides = (left, own, right)
    for pair in range(HEADS // 2):
        span = slice(pair * 2 * HDIM, (pair + 1) * 2 * HDIM)
        values = slice(width + span.start, width + span.stop)
        both = query[:, span].astype(jnp.float32)
        mixed = []
        for head in range(2):
            mine = low if head == 0 else jnp.logical_not(low)
            one = jnp.where(mine, both, 0.0).astype(jnp.bfloat16)
            scores = jnp.concatenate(
                [
                    lax.dot_general(
                        one,
                        side[:, span],
                        (((1,), (1,)), ((), ())),
                        preferred_element_type=jnp.float32,
                    )
                    for side in sides
                ],
                1,
            )
            scores = jnp.where(valid, scores * HDIM ** (-0.5), -1e30)
            weights = jnp.exp(scores - jnp.max(scores, -1, keepdims=True))
            probs = (weights / jnp.sum(weights, -1, keepdims=True)).astype(jnp.bfloat16)
            context = jnp.zeros((tokens, 2 * HDIM), jnp.float32)
            start = 0
            for side in sides:
                stop = start + side.shape[0]
                context += jnp.dot(
                    probs[:, start:stop], side[:, values], preferred_element_type=jnp.float32
                )
                start = stop
            mixed.append(context)
        ctx[:, span] = jnp.where(low, mixed[0], mixed[1]).astype(jnp.bfloat16)
    branch = jnp.dot(ctx[...], out_proj[...], preferred_element_type=jnp.float32)
    kept = (embed[...].astype(jnp.float32) + branch).astype(jnp.bfloat16)
    encoded[...] = kept
    post[...] = norm_rows(kept.astype(jnp.float32)).astype(jnp.bfloat16)


SMEM = pl.BlockSpec(memory_space=pltpu.SMEM)
VMEM = pl.BlockSpec(memory_space=pltpu.VMEM)
ANY = pl.BlockSpec(memory_space=pl.ANY)
HBM = pl.BlockSpec(memory_space=pltpu.HBM)


def room(mib):
    return pltpu.CompilerParams(vmem_limit_bytes=mib * 2**20)


def rows_of(*shape):
    return jax.ShapeDtypeStruct(shape, jnp.bfloat16)


def with_pieces(kernel, mib, place, operands, spreads, full, outs, scratch=(), first=()):
    flops = 2 * operands[0].shape[0] * full[0] * full[1]
    pieces, names = spreads
    copies = sum(len(stack) for stack in names)
    return pl.pallas_call(
        functools.partial(kernel, names),
        out_shape=outs,
        in_specs=[SMEM] + [VMEM] * len(operands) + [ANY] * (len(pieces) + len(first)),
        out_specs=jax.tree.map(lambda _: VMEM, outs),
        scratch_shapes=[
            *scratch,
            pltpu.VMEM(full, jnp.bfloat16),
            pltpu.SemaphoreType.DMA((copies,)),
        ],
        compiler_params=room(mib),
        cost_estimate=pl.CostEstimate(
            flops=4 * flops, bytes_accessed=4 * full[0] * full[1], transcendentals=0
        ),
    )(place, *operands, *pieces, *first)


def dense_device(
    spectral,
    recording_lengths,
    expert_ids,
    gate_weights,
    conv_weight,
    conv_proj,
    ln_gain,
    attn_in,
    attn_out,
    audio_proj,
    rms_gain,
    w_gate_up,
    w_down,
):
    devices = lax.axis_size("seq")
    zs, ys, cores = levels(devices)
    tokens = expert_ids.shape[0]
    experts = devices * w_down.shape[0]
    width = HEADS * HDIM
    channels = conv_weight.shape[1]
    bins = spectral.shape[1] // channels // 2
    me = lax.axis_index("seq")
    place = jnp.stack(
        [me // (ys * cores), me // cores % ys, me % cores, lax.axis_index("groups")]
    ).astype(jnp.int32)
    rim = shifted(spectral[-1:], "seq", 1)
    rows, wide, dim = attn_in.shape[0], attn_in.shape[1], conv_proj.shape[1]
    high, thin, broad = conv_proj.shape[0], attn_out.shape[0], audio_proj.shape[1]
    deep = -(-max(high + thin, 2 * rows) // 16) * 16
    packed = jnp.concatenate(
        [
            jnp.pad(jnp.concatenate([conv_proj, attn_out]), ((0, deep - high - thin), (0, 0))),
            jnp.pad(
                jnp.concatenate([jnp.pad(attn_in, ((0, 0), (0, broad - wide))), audio_proj]),
                ((0, deep - 2 * rows), (0, 0)),
            ),
        ],
        1,
    )
    late_full = lax.all_gather(packed, "seq", axis=0)
    audio_full = late_full[:, rows : 2 * rows, dim:].reshape(-1, broad)
    out_full = late_full[:, high : high + thin, :dim].reshape(-1, dim)
    conv_pieces = spread(conv_weight)
    gates = spread_gates(gate_table(expert_ids, gate_weights, experts))
    conv_act = with_pieces(
        conv_kernel,
        16,
        place,
        [spectral, rim],
        conv_pieces,
        (devices * conv_weight.shape[0], channels),
        rows_of(tokens, bins * channels),
        [pltpu.VMEM((3, (bins + 1) * tokens, 2 * channels), jnp.bfloat16)],
        gates,
    )
    embed, normed = pl.pallas_call(
        functools.partial(embed_kernel, high),
        out_shape=(rows_of(tokens, dim), rows_of(tokens, dim)),
        in_specs=[VMEM, VMEM, HBM],
        out_specs=(VMEM, VMEM),
        scratch_shapes=[
            pltpu.VMEM((devices * high, dim), jnp.bfloat16),
            pltpu.SemaphoreType.DMA((devices,)),
        ],
        compiler_params=room(46),
        cost_estimate=pl.CostEstimate(
            flops=4 * 10**9, bytes_accessed=5 * 10**6, transcendentals=0
        ),
    )(conv_act, ln_gain[None], late_full)
    query, key_rows = pl.pallas_call(
        functools.partial(qkv_kernel, dim),
        out_shape=(rows_of(tokens, width), rows_of(tokens, 2 * width)),
        in_specs=[VMEM, HBM],
        out_specs=(VMEM, VMEM),
        scratch_shapes=[
            pltpu.VMEM((devices * rows, wide), jnp.bfloat16),
            pltpu.SemaphoreType.DMA((devices,)),
        ],
        compiler_params=room(46),
        cost_estimate=pl.CostEstimate(
            flops=4 * 10**9, bytes_accessed=5 * 10**6, transcendentals=0
        ),
    )(normed, late_full)
    left = shifted(key_rows[-WIN:], "seq", 1)
    right = shifted(key_rows[:WIN], "seq", -1)
    ends = jnp.cumsum(recording_lengths).astype(jnp.int32)
    weighted = (w_gate_up[0] * rms_gain[:, None]).astype(jnp.bfloat16)
    fused = jnp.dot(audio_full, weighted, preferred_element_type=jnp.float32)
    fused = fused.astype(jnp.bfloat16)
    encoded, post = pl.pallas_call(
        functools.partial(attend_kernel, devices * tokens),
        out_shape=(rows_of(tokens, dim), rows_of(tokens, dim)),
        in_specs=[SMEM, SMEM] + [VMEM] * 6 + [ANY],
        out_specs=(VMEM, VMEM),
        scratch_shapes=[pltpu.VMEM((tokens, width), jnp.bfloat16)],
        compiler_params=room(8),
        cost_estimate=pl.CostEstimate(
            flops=4 * 10**9, bytes_accessed=4 * 10**6, transcendentals=0
        ),
    )(ends, (me * tokens)[None].astype(jnp.int32), query, left, key_rows, right, embed, out_full, fused)
    audio_sum = jnp.dot(post, audio_full, preferred_element_type=jnp.float32)
    audio_embed = audio_sum.astype(jnp.bfloat16)
    power = jnp.mean(jnp.square(audio_embed.astype(jnp.float32)), -1, keepdims=True)
    scaled = (post.astype(jnp.float32) * lax.rsqrt(power + 1e-06)).astype(jnp.bfloat16)
    return dense_experts(audio_embed, scaled, gates, fused, w_down[0])


def routed_device(
    spectral,
    recording_lengths,
    expert_ids,
    gate_weights,
    conv_weight,
    conv_proj,
    ln_gain,
    attn_in,
    attn_out,
    audio_proj,
    rms_gain,
    w_gate_up,
    w_down,
):
    devices = lax.axis_size("seq")
    local_tokens = expert_ids.shape[0]
    topk = expert_ids.shape[1]
    experts = devices * w_down.shape[0]
    slots = local_tokens * topk // experts + 1
    width = HEADS * HDIM
    channels = conv_weight.shape[1]
    freq_in = spectral.shape[1] // channels
    freq_out = freq_in // 2
    thinker_width = audio_proj.shape[1]
    proj_full = lax.all_gather(audio_proj, "seq", axis=0, tiled=True)
    frame_rim = shifted(spectral[-1:], "seq", 1)
    extended = jnp.concatenate([frame_rim, spectral], 0).reshape(
        2 * local_tokens + 1, freq_in, channels
    )
    extended = jnp.pad(extended, ((0, 0), (1, 0), (0, 0)))
    tap_list = []
    for across in range(3):
        row_set = extended[across : across + 2 * local_tokens : 2]
        for along in range(3):
            tap_list.append(row_set[:, along : along + freq_in : 2, :])
    patches = jnp.concatenate(tap_list, 2).reshape(local_tokens * freq_out, 9 * channels)
    conv_sum = fold_with(patches, lax.all_gather(conv_weight, "seq", axis=0, tiled=True))
    conv_act = (
        jax.nn.gelu(conv_sum, approximate=False)
        .astype(jnp.bfloat16)
        .reshape(local_tokens, freq_out * channels)
    )
    embed_sum = fold_with(conv_act, lax.all_gather(conv_proj, "seq", axis=0, tiled=True))
    embed = embed_sum.astype(jnp.bfloat16)
    normed = (layer_norm(embed.astype(jnp.float32)) * ln_gain).astype(jnp.bfloat16)
    qkv_sum = fold_with(normed, lax.all_gather(attn_in, "seq", axis=0, tiled=True))
    qkv = qkv_sum.astype(jnp.bfloat16)
    key_rows = padded(qkv[:, width:], (("seq", 0),), WIN)
    ends = jnp.cumsum(recording_lengths)
    first = lax.axis_index("seq") * local_tokens
    query_pos = first + jnp.arange(local_tokens, dtype=jnp.int32)
    key_pos = first - WIN + jnp.arange(local_tokens + 2 * WIN, dtype=jnp.int32)
    context = attend(qkv[:, :width], key_rows, query_pos, key_pos, ends, devices * local_tokens)
    branch_sum = fold_with(context, lax.all_gather(attn_out, "seq", axis=0, tiled=True))
    encoded = (embed.astype(jnp.float32) + branch_sum).astype(jnp.bfloat16)
    post = layer_norm(encoded.astype(jnp.float32)).astype(jnp.bfloat16)
    audio_embed = jnp.dot(post, proj_full, preferred_element_type=jnp.float32).astype(jnp.bfloat16)
    flat_ids = expert_ids.reshape(-1)
    onehot = (flat_ids[:, None] == jnp.arange(experts, dtype=jnp.int32)[None, :]).astype(jnp.int32)
    before = jnp.cumsum(onehot, 0) - onehot
    position = jnp.sum(before * onehot, 1)
    slot_index = flat_ids * slots + position
    owner = jnp.full((experts * slots,), local_tokens * topk, jnp.int32)
    owner = owner.at[slot_index].set(jnp.arange(local_tokens * topk, dtype=jnp.int32))
    owner_rows = owner // topk
    gate_up_local = w_gate_up[0]
    down_local = w_down[0]
    sent_rows = rms_norm(audio_embed, rms_gain)
    padded_rows = jnp.concatenate([sent_rows, jnp.zeros((1, sent_rows.shape[1]), jnp.bfloat16)], 0)
    send_buffer = padded_rows[owner_rows].reshape(experts, slots, sent_rows.shape[1])
    received = lax.all_to_all(send_buffer, "seq", split_axis=0, concat_axis=0, tiled=True)
    rows = received.reshape(-1, received.shape[-1])
    result = expert_ffn(rows, gate_up_local, down_local)
    results = result.reshape(received.shape[0], received.shape[1], thinker_width)
    returned = lax.all_to_all(results, "seq", split_axis=0, concat_axis=0, tiled=True)
    picked = returned.reshape(experts * slots, thinker_width)[slot_index].reshape(
        local_tokens, topk, thinker_width
    )
    expert_sum = jnp.sum(picked * gate_weights[:, :, None], 1)
    return (audio_embed.astype(jnp.float32) + expert_sum).astype(jnp.bfloat16)


def on_device(*arrays):
    devices = lax.axis_size("seq")
    experts, topk = devices * arrays[12].shape[0], arrays[2].shape[1]
    if experts <= 2 * topk and devices % 2 == 0:
        return dense_device(*arrays)
    return routed_device(*arrays)


def solution(mesh):
    placed = (
        P(("groups", "seq"), None),
        P("groups"),
        P(("groups", "seq"), None),
        P(("groups", "seq"), None),
        P("seq", None),
        P("seq", None),
        P(),
        P("seq", None),
        P("seq", None),
        P("seq", None),
        P(),
        P("seq", None, None),
        P("seq", None, None),
    )
    return jax.shard_map(
        on_device, mesh=mesh, in_specs=placed, out_specs=P(("groups", "seq"), None), check_vma=False
    )
```

```python
import functools

import jax
import jax.numpy as jnp
from jax import lax
from jax.experimental import pallas as pl
from jax.experimental.pallas import tpu as pltpu
from jax.sharding import PartitionSpec as P

HEADS = 10
HDIM = 64
WIN = 128


def shifted(block, axis, distance):
    devices = range(lax.axis_size(axis))
    route = [(i - distance, i) for i in devices if i - distance in devices]
    return lax.ppermute(block, axis, route)


def padded(cells, sides, width):
    for axis, dim in sides:
        count = lax.axis_size(axis)
        ends = count - 1
        head = lax.slice_in_dim(cells, 0, width, axis=dim)
        tail = lax.slice_in_dim(cells, cells.shape[dim] - width, cells.shape[dim], axis=dim)
        cells = jnp.concatenate(
            [
                lax.ppermute(tail, axis, [(i, (i + 1) % count) for i in range(ends)]),
                cells,
                lax.ppermute(head, axis, [((i + 1) % count, i) for i in range(ends)]),
            ],
            axis=dim,
        )
    return cells


def layer_norm(values):
    mean = jnp.mean(values, -1, keepdims=True)
    centered = values - mean
    variance = jnp.mean(centered * centered, -1, keepdims=True)
    return centered * lax.rsqrt(variance + 1e-05)


def rms_norm(values, gain):
    scaled = values.astype(jnp.float32)
    power = jnp.mean(scaled * scaled, -1, keepdims=True)
    return (scaled * lax.rsqrt(power + 1e-06) * gain).astype(jnp.bfloat16)


def recording_of(positions, ends):
    return jnp.sum((positions[:, None] >= ends[None, :]).astype(jnp.int32), 1)


def attend(query_rows, key_rows, query_pos, key_pos, ends, total):
    width = HEADS * HDIM
    count = query_rows.shape[0]
    keys_count = key_rows.shape[0]
    query = query_rows.reshape(count, HEADS, HDIM)
    keys = key_rows[:, :width].reshape(keys_count, HEADS, HDIM)
    values = key_rows[:, width:].reshape(keys_count, HEADS, HDIM)
    scores = jnp.einsum("qhd,khd->hqk", query, keys, preferred_element_type=jnp.float32) * HDIM ** (
        -0.5
    )
    same = recording_of(query_pos, ends)[:, None] == recording_of(key_pos, ends)[None, :]
    near = jnp.abs(query_pos[:, None] - key_pos[None, :]) <= WIN
    inside = (key_pos >= 0) & (key_pos < total)
    valid = same & near & inside[None, :]
    scores = jnp.where(valid[None], scores, -1e30)
    top = jnp.max(scores, -1, keepdims=True)
    weights = jnp.exp(scores - top)
    probs = (weights / jnp.sum(weights, -1, keepdims=True)).astype(jnp.bfloat16)
    context = jnp.einsum("hqk,khd->qhd", probs, values, preferred_element_type=jnp.float32)
    return context.reshape(count, width).astype(jnp.bfloat16)


def expert_ffn(rows, gate_up, down):
    both = jnp.dot(rows, gate_up, preferred_element_type=jnp.float32)
    inner = down.shape[0]
    hidden = (jax.nn.silu(both[:, :inner]) * both[:, inner:]).astype(jnp.bfloat16)
    return jnp.dot(hidden, down, preferred_element_type=jnp.float32).astype(jnp.bfloat16)


def fold_with(left, piece):
    return jnp.dot(left, piece, preferred_element_type=jnp.float32)


def ring_step(block, stride, size):
    route = []
    for i in range(lax.axis_size("seq")):
        place = i // stride % size
        route.append((i, i + ((place + 1) % size - place) * stride))
    return lax.ppermute(block, "seq", route)


def levels(devices):
    core = 2
    rest = devices // core
    y = 1
    while (2 * y) * (2 * y) <= rest:
        y *= 2
    return rest // y, y, core


def gate_table(expert_ids, gate_weights, experts):
    named = expert_ids[None] == jnp.arange(experts, dtype=jnp.int32)[:, None, None]
    return jnp.sum(jnp.where(named, gate_weights[None], 0.0), -1)


def spread_gates(table):
    zs, ys, cores = levels(lax.axis_size("seq"))
    blocks = [table]
    for _ in range(zs - 1):
        blocks.append(ring_step(blocks[-1], ys * cores, zs))
    line = [jnp.stack(blocks)]
    for _ in range(ys - 1):
        line.append(ring_step(line[-1], cores, ys))
    both = jnp.stack(line)
    both = jnp.stack([both, ring_step(both, 1, cores)])
    mine = lax.dynamic_index_in_dim(both, lax.axis_index("seq"), 3, keepdims=False)
    return [mine[:, :, k].reshape(-1) for k in range(zs)]


def once(block, other):
    zero = 0.0 * other[(0,) * other.ndim].astype(jnp.float32)
    return (block.astype(jnp.float32) + zero).astype(block.dtype)


def dense_experts(audio_embed, scaled, gates, fused, down):
    devices = lax.axis_size("seq")
    zs, ys, cores = levels(devices)
    tokens = scaled.shape[0]
    inner = down.shape[0]
    width = down.shape[1]
    blocks = [scaled]
    for k in range(1, zs):
        sent = once(blocks[-1], fused) if k == 2 else blocks[-1]
        blocks.append(ring_step(sent, ys * cores, zs))
    totals, columns, carry = {}, {}, None

    def send(k):
        block = blocks[k]
        line = [block]
        for _ in range(ys - 1):
            line.append(ring_step(line[-1], cores, ys))
        pair = jnp.stack(line)
        return jnp.stack([pair, ring_step(pair, 1, cores)])

    theirs = None
    for k in [*range(1, zs), 0]:
        rows = send(k).reshape(-1, scaled.shape[1])
        weight = gates[k][:, None]
        both = jnp.dot(rows, fused, preferred_element_type=jnp.float32)
        hidden = (jax.nn.silu(both[:, :inner]) * both[:, inner:] * weight).astype(jnp.bfloat16)
        sums = jnp.dot(hidden, down, preferred_element_type=jnp.float32).astype(jnp.bfloat16)
        totals[k] = sums
        sums = sums.reshape(cores, ys, tokens, width)
        theirs = ring_step(sums[1], 1, cores)
        chip = sums[0].astype(jnp.float32) + theirs.astype(jnp.float32)
        column = chip[1 % ys]
        for dy in range(1, ys):
            moved = ring_step(column.astype(jnp.bfloat16), cores, ys)
            column = moved.astype(jnp.float32) + chip[(dy + 1) % ys]
        columns[k] = column
    for k in list(range(1, zs)) + [0]:
        column = columns[k]
        if carry is not None:
            column = column + carry.astype(jnp.float32)
        if k:
            carry = ring_step(column.astype(jnp.bfloat16), ys * cores, zs)
    return (audio_embed.astype(jnp.float32) + column).astype(jnp.bfloat16)


def hop(block, stride, size, distance):
    route = []
    for i in range(lax.axis_size("seq")):
        place = i // stride % size
        route.append((i, i + ((place + distance) % size - place) * stride))
    return lax.ppermute(block, "seq", route)


def after(block, *others):
    return lax.optimization_barrier((block, *others))[0]


def spread(block, halves=1, late=None):
    zs, ys, cores = levels(lax.axis_size("seq"))
    if halves > 1:
        rows = block.shape[0] // halves
        block = lax.dynamic_slice_in_dim(block, lax.axis_index("groups") * rows, rows, 0)
    far = [hop(block, ys * cores, zs, k) for k in range(1, zs)]
    side = [hop(block, cores, ys, j) for j in range(1, ys)]
    stacks = [jnp.stack([block, *side, *far])]
    names = [[(0, j, 0, 0) for j in range(ys)] + [(k, 0, 0, 0) for k in range(1, zs)]]
    for j in range(1, ys):
        stacks.append(hop(stacks[0][ys:], cores, ys, j))
        names.append([(k, j, 0, 0) for k in range(1, zs)])
    if halves > 1:
        for i in range(len(stacks)):
            stacks.append(lax.ppermute(stacks[i], "groups", [(0, 1), (1, 0)]))
            names.append([(k, j, 0, 1) for k, j, _, _ in names[i]])
    for i in range(len(stacks)):
        sent = stacks[i] if late is None else after(stacks[i], late())
        stacks.append(hop(sent, 1, cores, 1))
        names.append([(k, j, 1, dx) for k, j, _, dx in names[i]])
    return stacks, names


def put_in_place(names, place, pieces, full, sems):
    halves = 1 + max(name[3] for stack in names for name in stack)
    rows = pieces[0].shape[1]
    zs, ys, cores = levels(full.shape[0] // (halves * rows))
    z, y, core, group = place[0], place[1], place[2], place[3]
    copies = []
    for piece, stack in zip(pieces, names):
        for i, (k, dy, dc, dx) in enumerate(stack):
            index = lax.rem(z - k + zs, zs) * ys + lax.rem(y - dy + ys, ys)
            index = index * cores + lax.rem(core - dc + cores, cores)
            start = index * (rows * halves)
            if halves > 1:
                start = start + lax.rem(group - dx + halves, halves) * rows
            copies.append(
                pltpu.make_async_copy(
                    piece.at[i],
                    full.at[pl.ds(pl.multiple_of(start, rows), rows)],
                    sems.at[len(copies)],
                )
            )
    for copy in copies:
        copy.start()
    for copy in copies:
        copy.wait()


def norm_rows(values):
    mean = jnp.mean(values, -1, keepdims=True)
    centered = values - mean
    variance = jnp.mean(centered * centered, -1, keepdims=True)
    return centered * lax.rsqrt(variance + 1e-05)


def conv_kernel(names, place, frames, rim, *refs):
    pieces, (out, taps, weight, sems) = refs[: len(names)], refs[-4:]
    tokens = out.shape[0]
    channels = weight.shape[1]
    bins = out.shape[1] // channels
    row = lax.broadcasted_iota(jnp.int32, (tokens, 2 * tokens), 0)
    column = lax.broadcasted_iota(jnp.int32, (tokens, 2 * tokens), 1)
    first = lax.broadcasted_iota(jnp.int32, (tokens, 2 * channels), 0) == 0
    for a in range(3):
        pick = jnp.where(column == 2 * row + a - 1, 1.0, 0.0).astype(jnp.bfloat16)
        taps[a, :tokens, :] = jnp.zeros((tokens, 2 * channels), jnp.bfloat16)
        for f in range(bins):
            span = slice(2 * f * channels, 2 * (f + 1) * channels)
            part = jnp.dot(pick, frames[:, span], preferred_element_type=jnp.float32)
            if a == 0:
                part = jnp.where(first, rim[:, span].astype(jnp.float32), part)
            taps[a, (f + 1) * tokens : (f + 2) * tokens, :] = part.astype(jnp.bfloat16)
    put_in_place(names, place, pieces, weight, sems)
    half = bins // 2 * tokens
    for part in range(2):
        total = jnp.zeros((half, channels), jnp.float32)
        low = part * half
        for a in range(3):
            base = 3 * a * channels
            total += jnp.dot(
                taps[a, low + tokens : low + tokens + half, :],
                weight[base + channels : base + 3 * channels],
                preferred_element_type=jnp.float32,
            )
            total += jnp.dot(
                taps[a, low : low + half, channels:],
                weight[base : base + channels],
                preferred_element_type=jnp.float32,
            )
        act = (0.5 * total * (1.0 + lax.erf(total * 0.7071067811865476))).astype(jnp.bfloat16)
        for f in range(bins // 2):
            where = (part * (bins // 2) + f) * channels
            out[:, where : where + channels] = act[f * tokens : (f + 1) * tokens]


def fetch(gathered, rows, first, full, sems):
    copies = [
        pltpu.make_async_copy(
            gathered.at[i, :rows, first : first + full.shape[1]],
            full.at[i * rows : (i + 1) * rows],
            sems.at[i],
        )
        for i in range(gathered.shape[0])
    ]
    for copy in copies:
        copy.start()
    for copy in copies:
        copy.wait()


def embed_kernel(rows, act, gain, gathered, embed, normed, weight, sems):
    fetch(gathered, rows, 0, weight, sems)
    step = 256
    for low in range(0, embed.shape[1], step):
        span = slice(low, low + step)
        sums = jnp.dot(act[...], weight[:, span], preferred_element_type=jnp.float32)
        embed[:, span] = sums.astype(jnp.bfloat16)
    kept = embed[...].astype(jnp.float32)
    normed[...] = (norm_rows(kept) * gain[...]).astype(jnp.bfloat16)


def qkv_kernel(first, normed, gathered, query, key_rows, weight, sems):
    fetch(gathered, weight.shape[0] // gathered.shape[0], first, weight, sems)
    width = query.shape[1]
    query[...] = jnp.dot(
        normed[...], weight[:, :width], preferred_element_type=jnp.float32
    ).astype(jnp.bfloat16)
    key_rows[...] = jnp.dot(
        normed[...], weight[:, width:], preferred_element_type=jnp.float32
    ).astype(jnp.bfloat16)


def attend_kernel(total, ends, first, query, left, own, right, embed, out_proj, *refs):
    encoded, post, ctx = refs[-3:]
    tokens, width = query.shape
    reach = left.shape[0]
    keys = tokens + 2 * reach
    query_pos = first[0] + lax.broadcasted_iota(jnp.int32, (tokens, keys), 0)
    key_pos = first[0] - reach + lax.broadcasted_iota(jnp.int32, (tokens, keys), 1)
    query_rec = jnp.zeros((tokens, keys), jnp.int32)
    key_rec = jnp.zeros((tokens, keys), jnp.int32)
    for r in range(ends.shape[0]):
        query_rec += (query_pos >= ends[r]).astype(jnp.int32)
        key_rec += (key_pos >= ends[r]).astype(jnp.int32)
    near = jnp.abs(query_pos - key_pos) <= WIN
    valid = (query_rec == key_rec) & near & (key_pos >= 0) & (key_pos < total)
    low = lax.broadcasted_iota(jnp.int32, (tokens, 2 * HDIM), 1) < HDIM
    sides = (left, own, right)
    for pair in range(HEADS // 2):
        span = slice(pair * 2 * HDIM, (pair + 1) * 2 * HDIM)
        values = slice(width + span.start, width + span.stop)
        both = query[:, span].astype(jnp.float32)
        mixed = []
        for head in range(2):
            mine = low if head == 0 else jnp.logical_not(low)
            one = jnp.where(mine, both, 0.0).astype(jnp.bfloat16)
            scores = jnp.concatenate(
                [
                    lax.dot_general(
                        one,
                        side[:, span],
                        (((1,), (1,)), ((), ())),
                        preferred_element_type=jnp.float32,
                    )
                    for side in sides
                ],
                1,
            )
            scores = jnp.where(valid, scores * HDIM ** (-0.5), -1e30)
            weights = jnp.exp(scores - jnp.max(scores, -1, keepdims=True))
            probs = (weights / jnp.sum(weights, -1, keepdims=True)).astype(jnp.bfloat16)
            context = jnp.zeros((tokens, 2 * HDIM), jnp.float32)
            start = 0
            for side in sides:
                stop = start + side.shape[0]
                context += jnp.dot(
                    probs[:, start:stop], side[:, values], preferred_element_type=jnp.float32
                )
                start = stop
            mixed.append(context)
        ctx[:, span] = jnp.where(low, mixed[0], mixed[1]).astype(jnp.bfloat16)
    branch = jnp.dot(ctx[...], out_proj[...], preferred_element_type=jnp.float32)
    kept = (embed[...].astype(jnp.float32) + branch).astype(jnp.bfloat16)
    encoded[...] = kept
    post[...] = norm_rows(kept.astype(jnp.float32)).astype(jnp.bfloat16)


SMEM = pl.BlockSpec(memory_space=pltpu.SMEM)
VMEM = pl.BlockSpec(memory_space=pltpu.VMEM)
ANY = pl.BlockSpec(memory_space=pl.ANY)
HBM = pl.BlockSpec(memory_space=pltpu.HBM)


def room(mib):
    return pltpu.CompilerParams(vmem_limit_bytes=mib * 2**20)


def rows_of(*shape):
    return jax.ShapeDtypeStruct(shape, jnp.bfloat16)


def with_pieces(kernel, mib, place, operands, spreads, full, outs, scratch=(), first=()):
    flops = 2 * operands[0].shape[0] * full[0] * full[1]
    pieces, names = spreads
    copies = sum(len(stack) for stack in names)
    return pl.pallas_call(
        functools.partial(kernel, names),
        out_shape=outs,
        in_specs=[SMEM] + [VMEM] * len(operands) + [ANY] * (len(pieces) + len(first)),
        out_specs=jax.tree.map(lambda _: VMEM, outs),
        scratch_shapes=[
            *scratch,
            pltpu.VMEM(full, jnp.bfloat16),
            pltpu.SemaphoreType.DMA((copies,)),
        ],
        compiler_params=room(mib),
        cost_estimate=pl.CostEstimate(
            flops=4 * flops, bytes_accessed=4 * full[0] * full[1], transcendentals=0
        ),
    )(place, *operands, *pieces, *first)


def dense_device(
    spectral,
    recording_lengths,
    expert_ids,
    gate_weights,
    conv_weight,
    conv_proj,
    ln_gain,
    attn_in,
    attn_out,
    audio_proj,
    rms_gain,
    w_gate_up,
    w_down,
):
    devices = lax.axis_size("seq")
    zs, ys, cores = levels(devices)
    tokens = expert_ids.shape[0]
    experts = devices * w_down.shape[0]
    width = HEADS * HDIM
    channels = conv_weight.shape[1]
    bins = spectral.shape[1] // channels // 2
    me = lax.axis_index("seq")
    place = jnp.stack(
        [me // (ys * cores), me // cores % ys, me % cores, lax.axis_index("groups")]
    ).astype(jnp.int32)
    rim = shifted(spectral[-1:], "seq", 1)
    rows, wide, dim = attn_in.shape[0], attn_in.shape[1], conv_proj.shape[1]
    high, thin, broad = conv_proj.shape[0], attn_out.shape[0], audio_proj.shape[1]
    lanes = broad - wide
    head = 2 * rows - high
    spare = attn_out[head:].reshape(thin - head, -1, lanes).swapaxes(0, 1).reshape(rows, lanes)
    packed = jnp.concatenate(
        [
            jnp.concatenate([conv_proj, attn_out[:head]]),
            jnp.concatenate([jnp.concatenate([attn_in, spare], 1), audio_proj]),
        ],
        1,
    )
    late_full = lax.all_gather(packed, "seq", axis=0)
    audio_full = late_full[:, rows : 2 * rows, dim:].reshape(-1, broad)
    spare = late_full[:, :rows, dim + wide :].reshape(devices, -1, thin - head, lanes)
    spare = spare.swapaxes(1, 2).reshape(devices, thin - head, dim)
    out_full = jnp.concatenate([late_full[:, high : high + head, :dim], spare], 1).reshape(-1, dim)
    conv_pieces = spread(conv_weight)
    gates = spread_gates(gate_table(expert_ids, gate_weights, experts))
    conv_act = with_pieces(
        conv_kernel,
        16,
        place,
        [spectral, rim],
        conv_pieces,
        (devices * conv_weight.shape[0], channels),
        rows_of(tokens, bins * channels),
        [pltpu.VMEM((3, (bins + 1) * tokens, 2 * channels), jnp.bfloat16)],
        gates,
    )
    embed, normed = pl.pallas_call(
        functools.partial(embed_kernel, high),
        out_shape=(rows_of(tokens, dim), rows_of(tokens, dim)),
        in_specs=[VMEM, VMEM, HBM],
        out_specs=(VMEM, VMEM),
        scratch_shapes=[
            pltpu.VMEM((devices * high, dim), jnp.bfloat16),
            pltpu.SemaphoreType.DMA((devices,)),
        ],
        compiler_params=room(46),
        cost_estimate=pl.CostEstimate(
            flops=4 * 10**9, bytes_accessed=5 * 10**6, transcendentals=0
        ),
    )(conv_act, ln_gain[None], late_full)
    query, key_rows = pl.pallas_call(
        functools.partial(qkv_kernel, dim),
        out_shape=(rows_of(tokens, width), rows_of(tokens, 2 * width)),
        in_specs=[VMEM, HBM],
        out_specs=(VMEM, VMEM),
        scratch_shapes=[
            pltpu.VMEM((devices * rows, wide), jnp.bfloat16),
            pltpu.SemaphoreType.DMA((devices,)),
        ],
        compiler_params=room(46),
        cost_estimate=pl.CostEstimate(
            flops=4 * 10**9, bytes_accessed=5 * 10**6, transcendentals=0
        ),
    )(normed, late_full)
    left = shifted(key_rows[-WIN:], "seq", 1)
    right = shifted(key_rows[:WIN], "seq", -1)
    ends = jnp.cumsum(recording_lengths).astype(jnp.int32)
    weighted = (w_gate_up[0] * rms_gain[:, None]).astype(jnp.bfloat16)
    fused = jnp.dot(audio_full, weighted, preferred_element_type=jnp.float32)
    fused = fused.astype(jnp.bfloat16)
    encoded, post = pl.pallas_call(
        functools.partial(attend_kernel, devices * tokens),
        out_shape=(rows_of(tokens, dim), rows_of(tokens, dim)),
        in_specs=[SMEM, SMEM] + [VMEM] * 6,
        out_specs=(VMEM, VMEM),
        scratch_shapes=[pltpu.VMEM((tokens, width), jnp.bfloat16)],
        compiler_params=room(8),
        cost_estimate=pl.CostEstimate(
            flops=4 * 10**9, bytes_accessed=4 * 10**6, transcendentals=0
        ),
    )(ends, (me * tokens)[None].astype(jnp.int32), query, left, key_rows, right, embed, out_full)
    audio_sum = jnp.dot(post, audio_full, preferred_element_type=jnp.float32)
    audio_embed = audio_sum.astype(jnp.bfloat16)
    power = jnp.mean(jnp.square(audio_embed.astype(jnp.float32)), -1, keepdims=True)
    scaled = (post.astype(jnp.float32) * lax.rsqrt(power + 1e-06)).astype(jnp.bfloat16)
    return dense_experts(audio_embed, scaled, gates, fused, w_down[0])


def routed_device(
    spectral,
    recording_lengths,
    expert_ids,
    gate_weights,
    conv_weight,
    conv_proj,
    ln_gain,
    attn_in,
    attn_out,
    audio_proj,
    rms_gain,
    w_gate_up,
    w_down,
):
    devices = lax.axis_size("seq")
    local_tokens = expert_ids.shape[0]
    topk = expert_ids.shape[1]
    experts = devices * w_down.shape[0]
    slots = local_tokens * topk // experts + 1
    width = HEADS * HDIM
    channels = conv_weight.shape[1]
    freq_in = spectral.shape[1] // channels
    freq_out = freq_in // 2
    thinker_width = audio_proj.shape[1]
    proj_full = lax.all_gather(audio_proj, "seq", axis=0, tiled=True)
    frame_rim = shifted(spectral[-1:], "seq", 1)
    extended = jnp.concatenate([frame_rim, spectral], 0).reshape(
        2 * local_tokens + 1, freq_in, channels
    )
    extended = jnp.pad(extended, ((0, 0), (1, 0), (0, 0)))
    tap_list = []
    for across in range(3):
        row_set = extended[across : across + 2 * local_tokens : 2]
        for along in range(3):
            tap_list.append(row_set[:, along : along + freq_in : 2, :])
    patches = jnp.concatenate(tap_list, 2).reshape(local_tokens * freq_out, 9 * channels)
    conv_sum = fold_with(patches, lax.all_gather(conv_weight, "seq", axis=0, tiled=True))
    conv_act = (
        jax.nn.gelu(conv_sum, approximate=False)
        .astype(jnp.bfloat16)
        .reshape(local_tokens, freq_out * channels)
    )
    embed_sum = fold_with(conv_act, lax.all_gather(conv_proj, "seq", axis=0, tiled=True))
    embed = embed_sum.astype(jnp.bfloat16)
    normed = (layer_norm(embed.astype(jnp.float32)) * ln_gain).astype(jnp.bfloat16)
    qkv_sum = fold_with(normed, lax.all_gather(attn_in, "seq", axis=0, tiled=True))
    qkv = qkv_sum.astype(jnp.bfloat16)
    key_rows = padded(qkv[:, width:], (("seq", 0),), WIN)
    ends = jnp.cumsum(recording_lengths)
    first = lax.axis_index("seq") * local_tokens
    query_pos = first + jnp.arange(local_tokens, dtype=jnp.int32)
    key_pos = first - WIN + jnp.arange(local_tokens + 2 * WIN, dtype=jnp.int32)
    context = attend(qkv[:, :width], key_rows, query_pos, key_pos, ends, devices * local_tokens)
    branch_sum = fold_with(context, lax.all_gather(attn_out, "seq", axis=0, tiled=True))
    encoded = (embed.astype(jnp.float32) + branch_sum).astype(jnp.bfloat16)
    post = layer_norm(encoded.astype(jnp.float32)).astype(jnp.bfloat16)
    audio_embed = jnp.dot(post, proj_full, preferred_element_type=jnp.float32).astype(jnp.bfloat16)
    flat_ids = expert_ids.reshape(-1)
    onehot = (flat_ids[:, None] == jnp.arange(experts, dtype=jnp.int32)[None, :]).astype(jnp.int32)
    before = jnp.cumsum(onehot, 0) - onehot
    position = jnp.sum(before * onehot, 1)
    slot_index = flat_ids * slots + position
    owner = jnp.full((experts * slots,), local_tokens * topk, jnp.int32)
    owner = owner.at[slot_index].set(jnp.arange(local_tokens * topk, dtype=jnp.int32))
    owner_rows = owner // topk
    gate_up_local = w_gate_up[0]
    down_local = w_down[0]
    sent_rows = rms_norm(audio_embed, rms_gain)
    padded_rows = jnp.concatenate([sent_rows, jnp.zeros((1, sent_rows.shape[1]), jnp.bfloat16)], 0)
    send_buffer = padded_rows[owner_rows].reshape(experts, slots, sent_rows.shape[1])
    received = lax.all_to_all(send_buffer, "seq", split_axis=0, concat_axis=0, tiled=True)
    rows = received.reshape(-1, received.shape[-1])
    result = expert_ffn(rows, gate_up_local, down_local)
    results = result.reshape(received.shape[0], received.shape[1], thinker_width)
    returned = lax.all_to_all(results, "seq", split_axis=0, concat_axis=0, tiled=True)
    picked = returned.reshape(experts * slots, thinker_width)[slot_index].reshape(
        local_tokens, topk, thinker_width
    )
    expert_sum = jnp.sum(picked * gate_weights[:, :, None], 1)
    return (audio_embed.astype(jnp.float32) + expert_sum).astype(jnp.bfloat16)


def on_device(*arrays):
    devices = lax.axis_size("seq")
    experts, topk = devices * arrays[12].shape[0], arrays[2].shape[1]
    if experts <= 2 * topk and devices % 2 == 0:
        return dense_device(*arrays)
    return routed_device(*arrays)


def solution(mesh):
    placed = (
        P(("groups", "seq"), None),
        P("groups"),
        P(("groups", "seq"), None),
        P(("groups", "seq"), None),
        P("seq", None),
        P("seq", None),
        P(),
        P("seq", None),
        P("seq", None),
        P("seq", None),
        P(),
        P("seq", None, None),
        P("seq", None, None),
    )
    return jax.shard_map(
        on_device, mesh=mesh, in_specs=placed, out_specs=P(("groups", "seq"), None), check_vma=False
    )
```

```python
import functools

import jax
import jax.numpy as jnp
from jax import lax
from jax.experimental import pallas as pl
from jax.experimental.pallas import tpu as pltpu
from jax.sharding import PartitionSpec as P

HEADS = 10
HDIM = 64
WIN = 128


def shifted(block, axis, distance):
    devices = range(lax.axis_size(axis))
    route = [(i - distance, i) for i in devices if i - distance in devices]
    return lax.ppermute(block, axis, route)


def padded(cells, sides, width):
    for axis, dim in sides:
        count = lax.axis_size(axis)
        ends = count - 1
        head = lax.slice_in_dim(cells, 0, width, axis=dim)
        tail = lax.slice_in_dim(cells, cells.shape[dim] - width, cells.shape[dim], axis=dim)
        cells = jnp.concatenate(
            [
                lax.ppermute(tail, axis, [(i, (i + 1) % count) for i in range(ends)]),
                cells,
                lax.ppermute(head, axis, [((i + 1) % count, i) for i in range(ends)]),
            ],
            axis=dim,
        )
    return cells


def layer_norm(values):
    mean = jnp.mean(values, -1, keepdims=True)
    centered = values - mean
    variance = jnp.mean(centered * centered, -1, keepdims=True)
    return centered * lax.rsqrt(variance + 1e-05)


def rms_norm(values, gain):
    scaled = values.astype(jnp.float32)
    power = jnp.mean(scaled * scaled, -1, keepdims=True)
    return (scaled * lax.rsqrt(power + 1e-06) * gain).astype(jnp.bfloat16)


def recording_of(positions, ends):
    return jnp.sum((positions[:, None] >= ends[None, :]).astype(jnp.int32), 1)


def attend(query_rows, key_rows, query_pos, key_pos, ends, total):
    width = HEADS * HDIM
    count = query_rows.shape[0]
    keys_count = key_rows.shape[0]
    query = query_rows.reshape(count, HEADS, HDIM)
    keys = key_rows[:, :width].reshape(keys_count, HEADS, HDIM)
    values = key_rows[:, width:].reshape(keys_count, HEADS, HDIM)
    scores = jnp.einsum("qhd,khd->hqk", query, keys, preferred_element_type=jnp.float32) * HDIM ** (
        -0.5
    )
    same = recording_of(query_pos, ends)[:, None] == recording_of(key_pos, ends)[None, :]
    near = jnp.abs(query_pos[:, None] - key_pos[None, :]) <= WIN
    inside = (key_pos >= 0) & (key_pos < total)
    valid = same & near & inside[None, :]
    scores = jnp.where(valid[None], scores, -1e30)
    top = jnp.max(scores, -1, keepdims=True)
    weights = jnp.exp(scores - top)
    probs = (weights / jnp.sum(weights, -1, keepdims=True)).astype(jnp.bfloat16)
    context = jnp.einsum("hqk,khd->qhd", probs, values, preferred_element_type=jnp.float32)
    return context.reshape(count, width).astype(jnp.bfloat16)


def expert_ffn(rows, gate_up, down):
    both = jnp.dot(rows, gate_up, preferred_element_type=jnp.float32)
    inner = down.shape[0]
    hidden = (jax.nn.silu(both[:, :inner]) * both[:, inner:]).astype(jnp.bfloat16)
    return jnp.dot(hidden, down, preferred_element_type=jnp.float32).astype(jnp.bfloat16)


def fold_with(left, piece):
    return jnp.dot(left, piece, preferred_element_type=jnp.float32)


def ring_step(block, stride, size):
    route = []
    for i in range(lax.axis_size("seq")):
        place = i // stride % size
        route.append((i, i + ((place + 1) % size - place) * stride))
    return lax.ppermute(block, "seq", route)


def levels(devices):
    core = 2
    rest = devices // core
    y = 1
    while (2 * y) * (2 * y) <= rest:
        y *= 2
    return rest // y, y, core


def gate_table(expert_ids, gate_weights, experts):
    named = expert_ids[None] == jnp.arange(experts, dtype=jnp.int32)[:, None, None]
    return jnp.sum(jnp.where(named, gate_weights[None], 0.0), -1)


def spread_gates(table):
    zs, ys, cores = levels(lax.axis_size("seq"))
    blocks = [table]
    for _ in range(zs - 1):
        blocks.append(ring_step(blocks[-1], ys * cores, zs))
    line = [jnp.stack(blocks)]
    for _ in range(ys - 1):
        line.append(ring_step(line[-1], cores, ys))
    both = jnp.stack(line)
    both = jnp.stack([both, ring_step(both, 1, cores)])
    mine = lax.dynamic_index_in_dim(both, lax.axis_index("seq"), 3, keepdims=False)
    return [mine[:, :, k].reshape(-1) for k in range(zs)]


def once(block, other):
    zero = 0.0 * other[(0,) * other.ndim].astype(jnp.float32)
    return (block.astype(jnp.float32) + zero).astype(block.dtype)


def dense_experts(audio_embed, scaled, gates, fused, down):
    devices = lax.axis_size("seq")
    zs, ys, cores = levels(devices)
    tokens = scaled.shape[0]
    inner = down.shape[0]
    width = down.shape[1]
    blocks = [scaled]
    early = ring_step(scaled, cores, ys)
    for k in range(1, zs):
        sent = once(once(blocks[-1], fused), early) if k == 2 else blocks[-1]
        blocks.append(ring_step(sent, ys * cores, zs))
    totals, columns, carry = {}, {}, None

    def send(k):
        block = blocks[k]
        line = [block]
        for dy in range(1, ys):
            known = k == 0 and dy == 1
            line.append(early if known else ring_step(line[-1], cores, ys))
        pair = jnp.stack(line)
        return jnp.stack([pair, ring_step(pair, 1, cores)])

    theirs = None
    for k in [*range(1, zs), 0]:
        rows = send(k).reshape(-1, scaled.shape[1])
        weight = gates[k][:, None]
        both = jnp.dot(rows, fused, preferred_element_type=jnp.float32)
        hidden = (jax.nn.silu(both[:, :inner]) * both[:, inner:] * weight).astype(jnp.bfloat16)
        sums = jnp.dot(hidden, down, preferred_element_type=jnp.float32).astype(jnp.bfloat16)
        totals[k] = sums
        sums = sums.reshape(cores, ys, tokens, width)
        theirs = ring_step(sums[1], 1, cores)
        chip = sums[0].astype(jnp.float32) + theirs.astype(jnp.float32)
        column = chip[1 % ys]
        for dy in range(1, ys):
            moved = ring_step(column.astype(jnp.bfloat16), cores, ys)
            column = moved.astype(jnp.float32) + chip[(dy + 1) % ys]
        columns[k] = column
    for k in list(range(1, zs)) + [0]:
        column = columns[k]
        if carry is not None:
            column = column + carry.astype(jnp.float32)
        if k:
            carry = ring_step(column.astype(jnp.bfloat16), ys * cores, zs)
    return (audio_embed.astype(jnp.float32) + column).astype(jnp.bfloat16)


def hop(block, stride, size, distance):
    route = []
    for i in range(lax.axis_size("seq")):
        place = i // stride % size
        route.append((i, i + ((place + distance) % size - place) * stride))
    return lax.ppermute(block, "seq", route)


def after(block, *others):
    return lax.optimization_barrier((block, *others))[0]


def spread(block, halves=1, late=None):
    zs, ys, cores = levels(lax.axis_size("seq"))
    if halves > 1:
        rows = block.shape[0] // halves
        block = lax.dynamic_slice_in_dim(block, lax.axis_index("groups") * rows, rows, 0)
    far = [hop(block, ys * cores, zs, k) for k in range(1, zs)]
    side = [hop(block, cores, ys, j) for j in range(1, ys)]
    stacks = [jnp.stack([block, *side, *far])]
    names = [[(0, j, 0, 0) for j in range(ys)] + [(k, 0, 0, 0) for k in range(1, zs)]]
    for j in range(1, ys):
        stacks.append(hop(stacks[0][ys:], cores, ys, j))
        names.append([(k, j, 0, 0) for k in range(1, zs)])
    if halves > 1:
        for i in range(len(stacks)):
            stacks.append(lax.ppermute(stacks[i], "groups", [(0, 1), (1, 0)]))
            names.append([(k, j, 0, 1) for k, j, _, _ in names[i]])
    for i in range(len(stacks)):
        sent = stacks[i] if late is None else after(stacks[i], late())
        stacks.append(hop(sent, 1, cores, 1))
        names.append([(k, j, 1, dx) for k, j, _, dx in names[i]])
    return stacks, names


def put_in_place(names, place, pieces, full, sems):
    halves = 1 + max(name[3] for stack in names for name in stack)
    rows = pieces[0].shape[1]
    zs, ys, cores = levels(full.shape[0] // (halves * rows))
    z, y, core, group = place[0], place[1], place[2], place[3]
    copies = []
    for piece, stack in zip(pieces, names):
        for i, (k, dy, dc, dx) in enumerate(stack):
            index = lax.rem(z - k + zs, zs) * ys + lax.rem(y - dy + ys, ys)
            index = index * cores + lax.rem(core - dc + cores, cores)
            start = index * (rows * halves)
            if halves > 1:
                start = start + lax.rem(group - dx + halves, halves) * rows
            copies.append(
                pltpu.make_async_copy(
                    piece.at[i],
                    full.at[pl.ds(pl.multiple_of(start, rows), rows)],
                    sems.at[len(copies)],
                )
            )
    for copy in copies:
        copy.start()
    for copy in copies:
        copy.wait()


def norm_rows(values):
    mean = jnp.mean(values, -1, keepdims=True)
    centered = values - mean
    variance = jnp.mean(centered * centered, -1, keepdims=True)
    return centered * lax.rsqrt(variance + 1e-05)


def conv_kernel(names, place, frames, rim, *refs):
    pieces, (out, taps, weight, sems) = refs[: len(names)], refs[-4:]
    tokens = out.shape[0]
    channels = weight.shape[1]
    bins = out.shape[1] // channels
    row = lax.broadcasted_iota(jnp.int32, (tokens, 2 * tokens), 0)
    column = lax.broadcasted_iota(jnp.int32, (tokens, 2 * tokens), 1)
    first = lax.broadcasted_iota(jnp.int32, (tokens, 2 * channels), 0) == 0
    for a in range(3):
        pick = jnp.where(column == 2 * row + a - 1, 1.0, 0.0).astype(jnp.bfloat16)
        taps[a, :tokens, :] = jnp.zeros((tokens, 2 * channels), jnp.bfloat16)
        for f in range(bins):
            span = slice(2 * f * channels, 2 * (f + 1) * channels)
            part = jnp.dot(pick, frames[:, span], preferred_element_type=jnp.float32)
            if a == 0:
                part = jnp.where(first, rim[:, span].astype(jnp.float32), part)
            taps[a, (f + 1) * tokens : (f + 2) * tokens, :] = part.astype(jnp.bfloat16)
    put_in_place(names, place, pieces, weight, sems)
    half = bins // 2 * tokens
    for part in range(2):
        total = jnp.zeros((half, channels), jnp.float32)
        low = part * half
        for a in range(3):
            base = 3 * a * channels
            total += jnp.dot(
                taps[a, low + tokens : low + tokens + half, :],
                weight[base + channels : base + 3 * channels],
                preferred_element_type=jnp.float32,
            )
            total += jnp.dot(
                taps[a, low : low + half, channels:],
                weight[base : base + channels],
                preferred_element_type=jnp.float32,
            )
        act = (0.5 * total * (1.0 + lax.erf(total * 0.7071067811865476))).astype(jnp.bfloat16)
        for f in range(bins // 2):
            where = (part * (bins // 2) + f) * channels
            out[:, where : where + channels] = act[f * tokens : (f + 1) * tokens]


def fetch(gathered, rows, first, full, sems):
    copies = [
        pltpu.make_async_copy(
            gathered.at[i, :rows, first : first + full.shape[1]],
            full.at[i * rows : (i + 1) * rows],
            sems.at[i],
        )
        for i in range(gathered.shape[0])
    ]
    for copy in copies:
        copy.start()
    return copies


def embed_kernel(
    rows, act, gain, gathered, embed, query, key_rows, weight, attn, weight_sems, attn_sems
):
    weight_copies = fetch(gathered, rows, 0, weight, weight_sems)
    attn_copies = fetch(
        gathered, attn.shape[0] // gathered.shape[0], weight.shape[1], attn, attn_sems
    )
    for copy in weight_copies:
        copy.wait()
    step = 256
    for low in range(0, embed.shape[1], step):
        span = slice(low, low + step)
        sums = jnp.dot(act[...], weight[:, span], preferred_element_type=jnp.float32)
        embed[:, span] = sums.astype(jnp.bfloat16)
    kept = embed[...].astype(jnp.float32)
    normed = (norm_rows(kept) * gain[...]).astype(jnp.bfloat16)
    for copy in attn_copies:
        copy.wait()
    width = query.shape[1]
    query[...] = jnp.dot(
        normed, attn[:, :width], preferred_element_type=jnp.float32
    ).astype(jnp.bfloat16)
    key_rows[...] = jnp.dot(
        normed, attn[:, width:], preferred_element_type=jnp.float32
    ).astype(jnp.bfloat16)


def attend_kernel(total, ends, first, query, left, own, right, embed, out_proj, *refs):
    encoded, post, ctx = refs[-3:]
    tokens, width = query.shape
    reach = left.shape[0]
    keys = tokens + 2 * reach
    query_pos = first[0] + lax.broadcasted_iota(jnp.int32, (tokens, keys), 0)
    key_pos = first[0] - reach + lax.broadcasted_iota(jnp.int32, (tokens, keys), 1)
    query_rec = jnp.zeros((tokens, keys), jnp.int32)
    key_rec = jnp.zeros((tokens, keys), jnp.int32)
    for r in range(ends.shape[0]):
        query_rec += (query_pos >= ends[r]).astype(jnp.int32)
        key_rec += (key_pos >= ends[r]).astype(jnp.int32)
    near = jnp.abs(query_pos - key_pos) <= WIN
    valid = (query_rec == key_rec) & near & (key_pos >= 0) & (key_pos < total)
    low = lax.broadcasted_iota(jnp.int32, (tokens, 2 * HDIM), 1) < HDIM
    sides = (left, own, right)
    for pair in range(HEADS // 2):
        span = slice(pair * 2 * HDIM, (pair + 1) * 2 * HDIM)
        values = slice(width + span.start, width + span.stop)
        both = query[:, span].astype(jnp.float32)
        mixed = []
        for head in range(2):
            mine = low if head == 0 else jnp.logical_not(low)
            one = jnp.where(mine, both, 0.0).astype(jnp.bfloat16)
            scores = jnp.concatenate(
                [
                    lax.dot_general(
                        one,
                        side[:, span],
                        (((1,), (1,)), ((), ())),
                        preferred_element_type=jnp.float32,
                    )
                    for side in sides
                ],
                1,
            )
            scores = jnp.where(valid, scores * HDIM ** (-0.5), -1e30)
            weights = jnp.exp(scores - jnp.max(scores, -1, keepdims=True))
            probs = (weights / jnp.sum(weights, -1, keepdims=True)).astype(jnp.bfloat16)
            context = jnp.zeros((tokens, 2 * HDIM), jnp.float32)
            start = 0
            for side in sides:
                stop = start + side.shape[0]
                context += jnp.dot(
                    probs[:, start:stop], side[:, values], preferred_element_type=jnp.float32
                )
                start = stop
            mixed.append(context)
        ctx[:, span] = jnp.where(low, mixed[0], mixed[1]).astype(jnp.bfloat16)
    branch = jnp.dot(ctx[...], out_proj[...], preferred_element_type=jnp.float32)
    kept = (embed[...].astype(jnp.float32) + branch).astype(jnp.bfloat16)
    encoded[...] = kept
    post[...] = norm_rows(kept.astype(jnp.float32)).astype(jnp.bfloat16)


SMEM = pl.BlockSpec(memory_space=pltpu.SMEM)
VMEM = pl.BlockSpec(memory_space=pltpu.VMEM)
ANY = pl.BlockSpec(memory_space=pl.ANY)
HBM = pl.BlockSpec(memory_space=pltpu.HBM)


def room(mib):
    return pltpu.CompilerParams(vmem_limit_bytes=mib * 2**20)


def rows_of(*shape):
    return jax.ShapeDtypeStruct(shape, jnp.bfloat16)


def with_pieces(kernel, mib, place, operands, spreads, full, outs, scratch=(), first=()):
    flops = 2 * operands[0].shape[0] * full[0] * full[1]
    pieces, names = spreads
    copies = sum(len(stack) for stack in names)
    return pl.pallas_call(
        functools.partial(kernel, names),
        out_shape=outs,
        in_specs=[SMEM] + [VMEM] * len(operands) + [ANY] * (len(pieces) + len(first)),
        out_specs=jax.tree.map(lambda _: VMEM, outs),
        scratch_shapes=[
            *scratch,
            pltpu.VMEM(full, jnp.bfloat16),
            pltpu.SemaphoreType.DMA((copies,)),
        ],
        compiler_params=room(mib),
        cost_estimate=pl.CostEstimate(
            flops=4 * flops, bytes_accessed=4 * full[0] * full[1], transcendentals=0
        ),
    )(place, *operands, *pieces, *first)


def dense_device(
    spectral,
    recording_lengths,
    expert_ids,
    gate_weights,
    conv_weight,
    conv_proj,
    ln_gain,
    attn_in,
    attn_out,
    audio_proj,
    rms_gain,
    w_gate_up,
    w_down,
):
    devices = lax.axis_size("seq")
    zs, ys, cores = levels(devices)
    tokens = expert_ids.shape[0]
    experts = devices * w_down.shape[0]
    width = HEADS * HDIM
    channels = conv_weight.shape[1]
    bins = spectral.shape[1] // channels // 2
    me = lax.axis_index("seq")
    place = jnp.stack(
        [me // (ys * cores), me // cores % ys, me % cores, lax.axis_index("groups")]
    ).astype(jnp.int32)
    rim = shifted(spectral[-1:], "seq", 1)
    rows, wide, dim = attn_in.shape[0], attn_in.shape[1], conv_proj.shape[1]
    high, thin, broad = conv_proj.shape[0], attn_out.shape[0], audio_proj.shape[1]
    lanes = broad - wide
    head = 2 * rows - high
    spare = attn_out[head:].reshape(thin - head, -1, lanes).swapaxes(0, 1).reshape(rows, lanes)
    packed = jnp.concatenate(
        [
            jnp.concatenate([conv_proj, attn_out[:head]]),
            jnp.concatenate([jnp.concatenate([attn_in, spare], 1), audio_proj]),
        ],
        1,
    )
    late_full = lax.all_gather(packed, "seq", axis=0)
    audio_full = late_full[:, rows : 2 * rows, dim:].reshape(-1, broad)
    spare = late_full[:, :rows, dim + wide :].reshape(devices, -1, thin - head, lanes)
    spare = spare.swapaxes(1, 2).reshape(devices, thin - head, dim)
    out_full = jnp.concatenate([late_full[:, high : high + head, :dim], spare], 1).reshape(-1, dim)
    conv_pieces = spread(conv_weight)
    gates = spread_gates(gate_table(expert_ids, gate_weights, experts))
    conv_act = with_pieces(
        conv_kernel,
        16,
        place,
        [spectral, rim],
        conv_pieces,
        (devices * conv_weight.shape[0], channels),
        rows_of(tokens, bins * channels),
        [pltpu.VMEM((3, (bins + 1) * tokens, 2 * channels), jnp.bfloat16)],
        gates,
    )
    embed, query, key_rows = pl.pallas_call(
        functools.partial(embed_kernel, high),
        out_shape=(rows_of(tokens, dim), rows_of(tokens, width), rows_of(tokens, 2 * width)),
        in_specs=[VMEM, VMEM, HBM],
        out_specs=(VMEM, VMEM, VMEM),
        scratch_shapes=[
            pltpu.VMEM((devices * high, dim), jnp.bfloat16),
            pltpu.VMEM((devices * rows, wide), jnp.bfloat16),
            pltpu.SemaphoreType.DMA((devices,)),
            pltpu.SemaphoreType.DMA((devices,)),
        ],
        compiler_params=room(46),
        cost_estimate=pl.CostEstimate(
            flops=8 * 10**9, bytes_accessed=10**7, transcendentals=0
        ),
    )(conv_act, ln_gain[None], late_full)
    left = shifted(key_rows[-WIN:], "seq", 1)
    right = shifted(key_rows[:WIN], "seq", -1)
    ends = jnp.cumsum(recording_lengths).astype(jnp.int32)
    weighted = (w_gate_up[0] * rms_gain[:, None]).astype(jnp.bfloat16)
    fused = jnp.dot(audio_full, weighted, preferred_element_type=jnp.float32)
    fused = fused.astype(jnp.bfloat16)
    encoded, post = pl.pallas_call(
        functools.partial(attend_kernel, devices * tokens),
        out_shape=(rows_of(tokens, dim), rows_of(tokens, dim)),
        in_specs=[SMEM, SMEM] + [VMEM] * 6,
        out_specs=(VMEM, VMEM),
        scratch_shapes=[pltpu.VMEM((tokens, width), jnp.bfloat16)],
        compiler_params=room(8),
        cost_estimate=pl.CostEstimate(
            flops=4 * 10**9, bytes_accessed=4 * 10**6, transcendentals=0
        ),
    )(ends, (me * tokens)[None].astype(jnp.int32), query, left, key_rows, right, embed, out_full)
    audio_sum = jnp.dot(post, audio_full, preferred_element_type=jnp.float32)
    audio_embed = audio_sum.astype(jnp.bfloat16)
    power = jnp.mean(jnp.square(audio_embed.astype(jnp.float32)), -1, keepdims=True)
    scaled = (post.astype(jnp.float32) * lax.rsqrt(power + 1e-06)).astype(jnp.bfloat16)
    return dense_experts(audio_embed, scaled, gates, fused, w_down[0])


def routed_device(
    spectral,
    recording_lengths,
    expert_ids,
    gate_weights,
    conv_weight,
    conv_proj,
    ln_gain,
    attn_in,
    attn_out,
    audio_proj,
    rms_gain,
    w_gate_up,
    w_down,
):
    devices = lax.axis_size("seq")
    local_tokens = expert_ids.shape[0]
    topk = expert_ids.shape[1]
    experts = devices * w_down.shape[0]
    slots = local_tokens * topk // experts + 1
    width = HEADS * HDIM
    channels = conv_weight.shape[1]
    freq_in = spectral.shape[1] // channels
    freq_out = freq_in // 2
    thinker_width = audio_proj.shape[1]
    proj_full = lax.all_gather(audio_proj, "seq", axis=0, tiled=True)
    frame_rim = shifted(spectral[-1:], "seq", 1)
    extended = jnp.concatenate([frame_rim, spectral], 0).reshape(
        2 * local_tokens + 1, freq_in, channels
    )
    extended = jnp.pad(extended, ((0, 0), (1, 0), (0, 0)))
    tap_list = []
    for across in range(3):
        row_set = extended[across : across + 2 * local_tokens : 2]
        for along in range(3):
            tap_list.append(row_set[:, along : along + freq_in : 2, :])
    patches = jnp.concatenate(tap_list, 2).reshape(local_tokens * freq_out, 9 * channels)
    conv_sum = fold_with(patches, lax.all_gather(conv_weight, "seq", axis=0, tiled=True))
    conv_act = (
        jax.nn.gelu(conv_sum, approximate=False)
        .astype(jnp.bfloat16)
        .reshape(local_tokens, freq_out * channels)
    )
    embed_sum = fold_with(conv_act, lax.all_gather(conv_proj, "seq", axis=0, tiled=True))
    embed = embed_sum.astype(jnp.bfloat16)
    normed = (layer_norm(embed.astype(jnp.float32)) * ln_gain).astype(jnp.bfloat16)
    qkv_sum = fold_with(normed, lax.all_gather(attn_in, "seq", axis=0, tiled=True))
    qkv = qkv_sum.astype(jnp.bfloat16)
    key_rows = padded(qkv[:, width:], (("seq", 0),), WIN)
    ends = jnp.cumsum(recording_lengths)
    first = lax.axis_index("seq") * local_tokens
    query_pos = first + jnp.arange(local_tokens, dtype=jnp.int32)
    key_pos = first - WIN + jnp.arange(local_tokens + 2 * WIN, dtype=jnp.int32)
    context = attend(qkv[:, :width], key_rows, query_pos, key_pos, ends, devices * local_tokens)
    branch_sum = fold_with(context, lax.all_gather(attn_out, "seq", axis=0, tiled=True))
    encoded = (embed.astype(jnp.float32) + branch_sum).astype(jnp.bfloat16)
    post = layer_norm(encoded.astype(jnp.float32)).astype(jnp.bfloat16)
    audio_embed = jnp.dot(post, proj_full, preferred_element_type=jnp.float32).astype(jnp.bfloat16)
    flat_ids = expert_ids.reshape(-1)
    onehot = (flat_ids[:, None] == jnp.arange(experts, dtype=jnp.int32)[None, :]).astype(jnp.int32)
    before = jnp.cumsum(onehot, 0) - onehot
    position = jnp.sum(before * onehot, 1)
    slot_index = flat_ids * slots + position
    owner = jnp.full((experts * slots,), local_tokens * topk, jnp.int32)
    owner = owner.at[slot_index].set(jnp.arange(local_tokens * topk, dtype=jnp.int32))
    owner_rows = owner // topk
    gate_up_local = w_gate_up[0]
    down_local = w_down[0]
    sent_rows = rms_norm(audio_embed, rms_gain)
    padded_rows = jnp.concatenate([sent_rows, jnp.zeros((1, sent_rows.shape[1]), jnp.bfloat16)], 0)
    send_buffer = padded_rows[owner_rows].reshape(experts, slots, sent_rows.shape[1])
    received = lax.all_to_all(send_buffer, "seq", split_axis=0, concat_axis=0, tiled=True)
    rows = received.reshape(-1, received.shape[-1])
    result = expert_ffn(rows, gate_up_local, down_local)
    results = result.reshape(received.shape[0], received.shape[1], thinker_width)
    returned = lax.all_to_all(results, "seq", split_axis=0, concat_axis=0, tiled=True)
    picked = returned.reshape(experts * slots, thinker_width)[slot_index].reshape(
        local_tokens, topk, thinker_width
    )
    expert_sum = jnp.sum(picked * gate_weights[:, :, None], 1)
    return (audio_embed.astype(jnp.float32) + expert_sum).astype(jnp.bfloat16)


def on_device(*arrays):
    devices = lax.axis_size("seq")
    experts, topk = devices * arrays[12].shape[0], arrays[2].shape[1]
    if experts <= 2 * topk and devices % 2 == 0:
        return dense_device(*arrays)
    return routed_device(*arrays)


def solution(mesh):
    placed = (
        P(("groups", "seq"), None),
        P("groups"),
        P(("groups", "seq"), None),
        P(("groups", "seq"), None),
        P("seq", None),
        P("seq", None),
        P(),
        P("seq", None),
        P("seq", None),
        P("seq", None),
        P(),
        P("seq", None, None),
        P("seq", None, None),
    )
    return jax.shard_map(
        on_device, mesh=mesh, in_specs=placed, out_specs=P(("groups", "seq"), None), check_vma=False
    )
```

```python
import functools

import jax
import jax.numpy as jnp
from jax import lax
from jax.experimental import pallas as pl
from jax.experimental.pallas import tpu as pltpu
from jax.sharding import PartitionSpec as P

HEADS = 10
HDIM = 64
WIN = 128


def shifted(block, axis, distance):
    devices = range(lax.axis_size(axis))
    route = [(i - distance, i) for i in devices if i - distance in devices]
    return lax.ppermute(block, axis, route)


def padded(cells, sides, width):
    for axis, dim in sides:
        count = lax.axis_size(axis)
        ends = count - 1
        head = lax.slice_in_dim(cells, 0, width, axis=dim)
        tail = lax.slice_in_dim(cells, cells.shape[dim] - width, cells.shape[dim], axis=dim)
        cells = jnp.concatenate(
            [
                lax.ppermute(tail, axis, [(i, (i + 1) % count) for i in range(ends)]),
                cells,
                lax.ppermute(head, axis, [((i + 1) % count, i) for i in range(ends)]),
            ],
            axis=dim,
        )
    return cells


def layer_norm(values):
    mean = jnp.mean(values, -1, keepdims=True)
    centered = values - mean
    variance = jnp.mean(centered * centered, -1, keepdims=True)
    return centered * lax.rsqrt(variance + 1e-05)


def rms_norm(values, gain):
    scaled = values.astype(jnp.float32)
    power = jnp.mean(scaled * scaled, -1, keepdims=True)
    return (scaled * lax.rsqrt(power + 1e-06) * gain).astype(jnp.bfloat16)


def recording_of(positions, ends):
    return jnp.sum((positions[:, None] >= ends[None, :]).astype(jnp.int32), 1)


def attend(query_rows, key_rows, query_pos, key_pos, ends, total):
    width = HEADS * HDIM
    count = query_rows.shape[0]
    keys_count = key_rows.shape[0]
    query = query_rows.reshape(count, HEADS, HDIM)
    keys = key_rows[:, :width].reshape(keys_count, HEADS, HDIM)
    values = key_rows[:, width:].reshape(keys_count, HEADS, HDIM)
    scores = jnp.einsum("qhd,khd->hqk", query, keys, preferred_element_type=jnp.float32) * HDIM ** (
        -0.5
    )
    same = recording_of(query_pos, ends)[:, None] == recording_of(key_pos, ends)[None, :]
    near = jnp.abs(query_pos[:, None] - key_pos[None, :]) <= WIN
    inside = (key_pos >= 0) & (key_pos < total)
    valid = same & near & inside[None, :]
    scores = jnp.where(valid[None], scores, -1e30)
    top = jnp.max(scores, -1, keepdims=True)
    weights = jnp.exp(scores - top)
    probs = (weights / jnp.sum(weights, -1, keepdims=True)).astype(jnp.bfloat16)
    context = jnp.einsum("hqk,khd->qhd", probs, values, preferred_element_type=jnp.float32)
    return context.reshape(count, width).astype(jnp.bfloat16)


def expert_ffn(rows, gate_up, down):
    both = jnp.dot(rows, gate_up, preferred_element_type=jnp.float32)
    inner = down.shape[0]
    hidden = (jax.nn.silu(both[:, :inner]) * both[:, inner:]).astype(jnp.bfloat16)
    return jnp.dot(hidden, down, preferred_element_type=jnp.float32).astype(jnp.bfloat16)


def fold_with(left, piece):
    return jnp.dot(left, piece, preferred_element_type=jnp.float32)


def ring_step(block, stride, size):
    route = []
    for i in range(lax.axis_size("seq")):
        place = i // stride % size
        route.append((i, i + ((place + 1) % size - place) * stride))
    return lax.ppermute(block, "seq", route)


def levels(devices):
    core = 2
    rest = devices // core
    y = 1
    while (2 * y) * (2 * y) <= rest:
        y *= 2
    return rest // y, y, core


def gate_table(expert_ids, gate_weights, experts):
    named = expert_ids[None] == jnp.arange(experts, dtype=jnp.int32)[:, None, None]
    return jnp.sum(jnp.where(named, gate_weights[None], 0.0), -1)


def spread_gates(table):
    zs, ys, cores = levels(lax.axis_size("seq"))
    blocks = [table]
    for _ in range(zs - 1):
        blocks.append(ring_step(blocks[-1], ys * cores, zs))
    line = [jnp.stack(blocks)]
    for _ in range(ys - 1):
        line.append(ring_step(line[-1], cores, ys))
    both = jnp.stack(line)
    both = jnp.stack([both, ring_step(both, 1, cores)])
    mine = lax.dynamic_index_in_dim(both, lax.axis_index("seq"), 3, keepdims=False)
    return [mine[:, :, k].reshape(-1) for k in range(zs)]


def once(block, other):
    zero = 0.0 * other[(0,) * other.ndim].astype(jnp.float32)
    return (block.astype(jnp.float32) + zero).astype(block.dtype)


def dense_experts(audio_embed, scaled, gates, fused, down):
    devices = lax.axis_size("seq")
    zs, ys, cores = levels(devices)
    tokens = scaled.shape[0]
    inner = down.shape[0]
    width = down.shape[1]
    blocks = [scaled]
    early = ring_step(scaled, cores, ys)
    for k in range(1, zs):
        sent = once(once(blocks[-1], fused), early) if k == 2 else blocks[-1]
        blocks.append(ring_step(sent, ys * cores, zs))
    totals, columns, carry = {}, {}, None

    def send(k):
        block = blocks[k]
        line = [block]
        for dy in range(1, ys):
            known = k == 0 and dy == 1
            line.append(early if known else ring_step(line[-1], cores, ys))
        pair = jnp.stack(line)
        return jnp.stack([pair, ring_step(pair, 1, cores)])

    theirs = None
    for k in range(zs):
        rows = send(k).reshape(-1, scaled.shape[1])
        weight = gates[k][:, None]
        both = jnp.dot(rows, fused, preferred_element_type=jnp.float32)
        hidden = (jax.nn.silu(both[:, :inner]) * both[:, inner:] * weight).astype(jnp.bfloat16)
        sums = jnp.dot(hidden, down, preferred_element_type=jnp.float32).astype(jnp.bfloat16)
        totals[k] = sums
        sums = sums.reshape(cores, ys, tokens, width)
        theirs = ring_step(sums[1], 1, cores)
        chip = sums[0].astype(jnp.float32) + theirs.astype(jnp.float32)
        column = chip[1 % ys]
        for dy in range(1, ys):
            moved = ring_step(column.astype(jnp.bfloat16), cores, ys)
            column = moved.astype(jnp.float32) + chip[(dy + 1) % ys]
        columns[k] = column
    for k in list(range(1, zs)) + [0]:
        column = columns[k]
        if carry is not None:
            column = column + carry.astype(jnp.float32)
        if k:
            carry = ring_step(column.astype(jnp.bfloat16), ys * cores, zs)
    return (audio_embed.astype(jnp.float32) + column).astype(jnp.bfloat16)


def hop(block, stride, size, distance):
    route = []
    for i in range(lax.axis_size("seq")):
        place = i // stride % size
        route.append((i, i + ((place + distance) % size - place) * stride))
    return lax.ppermute(block, "seq", route)


def after(block, *others):
    return lax.optimization_barrier((block, *others))[0]


def spread(block, halves=1, late=None):
    zs, ys, cores = levels(lax.axis_size("seq"))
    if halves > 1:
        rows = block.shape[0] // halves
        block = lax.dynamic_slice_in_dim(block, lax.axis_index("groups") * rows, rows, 0)
    far = [hop(block, ys * cores, zs, k) for k in range(1, zs)]
    side = [hop(block, cores, ys, j) for j in range(1, ys)]
    stacks = [jnp.stack([block, *side, *far])]
    names = [[(0, j, 0, 0) for j in range(ys)] + [(k, 0, 0, 0) for k in range(1, zs)]]
    for j in range(1, ys):
        stacks.append(hop(stacks[0][ys:], cores, ys, j))
        names.append([(k, j, 0, 0) for k in range(1, zs)])
    if halves > 1:
        for i in range(len(stacks)):
            stacks.append(lax.ppermute(stacks[i], "groups", [(0, 1), (1, 0)]))
            names.append([(k, j, 0, 1) for k, j, _, _ in names[i]])
    for i in range(len(stacks)):
        sent = stacks[i] if late is None else after(stacks[i], late())
        stacks.append(hop(sent, 1, cores, 1))
        names.append([(k, j, 1, dx) for k, j, _, dx in names[i]])
    return stacks, names


def put_in_place(names, place, pieces, full, sems):
    halves = 1 + max(name[3] for stack in names for name in stack)
    rows = pieces[0].shape[1]
    zs, ys, cores = levels(full.shape[0] // (halves * rows))
    z, y, core, group = place[0], place[1], place[2], place[3]
    copies = []
    for piece, stack in zip(pieces, names):
        for i, (k, dy, dc, dx) in enumerate(stack):
            index = lax.rem(z - k + zs, zs) * ys + lax.rem(y - dy + ys, ys)
            index = index * cores + lax.rem(core - dc + cores, cores)
            start = index * (rows * halves)
            if halves > 1:
                start = start + lax.rem(group - dx + halves, halves) * rows
            copies.append(
                pltpu.make_async_copy(
                    piece.at[i],
                    full.at[pl.ds(pl.multiple_of(start, rows), rows)],
                    sems.at[len(copies)],
                )
            )
    for copy in copies:
        copy.start()
    for copy in copies:
        copy.wait()


def norm_rows(values):
    mean = jnp.mean(values, -1, keepdims=True)
    centered = values - mean
    variance = jnp.mean(centered * centered, -1, keepdims=True)
    return centered * lax.rsqrt(variance + 1e-05)


def conv_kernel(names, place, frames, rim, *refs):
    pieces, (out, taps, weight, sems) = refs[: len(names)], refs[-4:]
    tokens = out.shape[0]
    channels = weight.shape[1]
    bins = out.shape[1] // channels
    row = lax.broadcasted_iota(jnp.int32, (tokens, 2 * tokens), 0)
    column = lax.broadcasted_iota(jnp.int32, (tokens, 2 * tokens), 1)
    first = lax.broadcasted_iota(jnp.int32, (tokens, 2 * channels), 0) == 0
    for a in range(3):
        pick = jnp.where(column == 2 * row + a - 1, 1.0, 0.0).astype(jnp.bfloat16)
        taps[a, :tokens, :] = jnp.zeros((tokens, 2 * channels), jnp.bfloat16)
        for f in range(bins):
            span = slice(2 * f * channels, 2 * (f + 1) * channels)
            part = jnp.dot(pick, frames[:, span], preferred_element_type=jnp.float32)
            if a == 0:
                part = jnp.where(first, rim[:, span].astype(jnp.float32), part)
            taps[a, (f + 1) * tokens : (f + 2) * tokens, :] = part.astype(jnp.bfloat16)
    put_in_place(names, place, pieces, weight, sems)
    half = bins // 2 * tokens
    for part in range(2):
        total = jnp.zeros((half, channels), jnp.float32)
        low = part * half
        for a in range(3):
            base = 3 * a * channels
            total += jnp.dot(
                taps[a, low + tokens : low + tokens + half, :],
                weight[base + channels : base + 3 * channels],
                preferred_element_type=jnp.float32,
            )
            total += jnp.dot(
                taps[a, low : low + half, channels:],
                weight[base : base + channels],
                preferred_element_type=jnp.float32,
            )
        act = (0.5 * total * (1.0 + lax.erf(total * 0.7071067811865476))).astype(jnp.bfloat16)
        for f in range(bins // 2):
            where = (part * (bins // 2) + f) * channels
            out[:, where : where + channels] = act[f * tokens : (f + 1) * tokens]


def fetch(gathered, rows, first, full, sems):
    copies = [
        pltpu.make_async_copy(
            gathered.at[i, :rows, first : first + full.shape[1]],
            full.at[i * rows : (i + 1) * rows],
            sems.at[i],
        )
        for i in range(gathered.shape[0])
    ]
    for copy in copies:
        copy.start()
    return copies


def embed_kernel(
    rows, act, gain, gathered, embed, query, key_rows, weight, attn, weight_sems, attn_sems
):
    weight_copies = fetch(gathered, rows, 0, weight, weight_sems)
    attn_copies = fetch(
        gathered, attn.shape[0] // gathered.shape[0], weight.shape[1], attn, attn_sems
    )
    for copy in weight_copies:
        copy.wait()
    step = 256
    for low in range(0, embed.shape[1], step):
        span = slice(low, low + step)
        sums = jnp.dot(act[...], weight[:, span], preferred_element_type=jnp.float32)
        embed[:, span] = sums.astype(jnp.bfloat16)
    kept = embed[...].astype(jnp.float32)
    normed = (norm_rows(kept) * gain[...]).astype(jnp.bfloat16)
    for copy in attn_copies:
        copy.wait()
    width = query.shape[1]
    query[...] = jnp.dot(
        normed, attn[:, :width], preferred_element_type=jnp.float32
    ).astype(jnp.bfloat16)
    key_rows[...] = jnp.dot(
        normed, attn[:, width:], preferred_element_type=jnp.float32
    ).astype(jnp.bfloat16)


def attend_kernel(total, ends, first, query, left, own, right, embed, out_proj, *refs):
    encoded, post, ctx = refs[-3:]
    tokens, width = query.shape
    reach = left.shape[0]
    keys = tokens + 2 * reach
    query_pos = first[0] + lax.broadcasted_iota(jnp.int32, (tokens, keys), 0)
    key_pos = first[0] - reach + lax.broadcasted_iota(jnp.int32, (tokens, keys), 1)
    query_rec = jnp.zeros((tokens, keys), jnp.int32)
    key_rec = jnp.zeros((tokens, keys), jnp.int32)
    for r in range(ends.shape[0]):
        query_rec += (query_pos >= ends[r]).astype(jnp.int32)
        key_rec += (key_pos >= ends[r]).astype(jnp.int32)
    near = jnp.abs(query_pos - key_pos) <= WIN
    valid = (query_rec == key_rec) & near & (key_pos >= 0) & (key_pos < total)
    low = lax.broadcasted_iota(jnp.int32, (tokens, 2 * HDIM), 1) < HDIM
    sides = (left, own, right)
    for pair in range(HEADS // 2):
        span = slice(pair * 2 * HDIM, (pair + 1) * 2 * HDIM)
        values = slice(width + span.start, width + span.stop)
        both = query[:, span].astype(jnp.float32)
        mixed = []
        for head in range(2):
            mine = low if head == 0 else jnp.logical_not(low)
            one = jnp.where(mine, both, 0.0).astype(jnp.bfloat16)
            scores = jnp.concatenate(
                [
                    lax.dot_general(
                        one,
                        side[:, span],
                        (((1,), (1,)), ((), ())),
                        preferred_element_type=jnp.float32,
                    )
                    for side in sides
                ],
                1,
            )
            scores = jnp.where(valid, scores * HDIM ** (-0.5), -1e30)
            weights = jnp.exp(scores - jnp.max(scores, -1, keepdims=True))
            probs = (weights / jnp.sum(weights, -1, keepdims=True)).astype(jnp.bfloat16)
            context = jnp.zeros((tokens, 2 * HDIM), jnp.float32)
            start = 0
            for side in sides:
                stop = start + side.shape[0]
                context += jnp.dot(
                    probs[:, start:stop], side[:, values], preferred_element_type=jnp.float32
                )
                start = stop
            mixed.append(context)
        ctx[:, span] = jnp.where(low, mixed[0], mixed[1]).astype(jnp.bfloat16)
    branch = jnp.dot(ctx[...], out_proj[...], preferred_element_type=jnp.float32)
    kept = (embed[...].astype(jnp.float32) + branch).astype(jnp.bfloat16)
    encoded[...] = kept
    post[...] = norm_rows(kept.astype(jnp.float32)).astype(jnp.bfloat16)


SMEM = pl.BlockSpec(memory_space=pltpu.SMEM)
VMEM = pl.BlockSpec(memory_space=pltpu.VMEM)
ANY = pl.BlockSpec(memory_space=pl.ANY)
HBM = pl.BlockSpec(memory_space=pltpu.HBM)


def room(mib):
    return pltpu.CompilerParams(vmem_limit_bytes=mib * 2**20)


def rows_of(*shape):
    return jax.ShapeDtypeStruct(shape, jnp.bfloat16)


def with_pieces(kernel, mib, place, operands, spreads, full, outs, scratch=(), first=()):
    flops = 2 * operands[0].shape[0] * full[0] * full[1]
    pieces, names = spreads
    copies = sum(len(stack) for stack in names)
    return pl.pallas_call(
        functools.partial(kernel, names),
        out_shape=outs,
        in_specs=[SMEM] + [VMEM] * len(operands) + [ANY] * (len(pieces) + len(first)),
        out_specs=jax.tree.map(lambda _: VMEM, outs),
        scratch_shapes=[
            *scratch,
            pltpu.VMEM(full, jnp.bfloat16),
            pltpu.SemaphoreType.DMA((copies,)),
        ],
        compiler_params=room(mib),
        cost_estimate=pl.CostEstimate(
            flops=4 * flops, bytes_accessed=4 * full[0] * full[1], transcendentals=0
        ),
    )(place, *operands, *pieces, *first)


def dense_device(
    spectral,
    recording_lengths,
    expert_ids,
    gate_weights,
    conv_weight,
    conv_proj,
    ln_gain,
    attn_in,
    attn_out,
    audio_proj,
    rms_gain,
    w_gate_up,
    w_down,
):
    devices = lax.axis_size("seq")
    zs, ys, cores = levels(devices)
    tokens = expert_ids.shape[0]
    experts = devices * w_down.shape[0]
    width = HEADS * HDIM
    channels = conv_weight.shape[1]
    bins = spectral.shape[1] // channels // 2
    me = lax.axis_index("seq")
    place = jnp.stack(
        [me // (ys * cores), me // cores % ys, me % cores, lax.axis_index("groups")]
    ).astype(jnp.int32)
    rim = shifted(spectral[-1:], "seq", 1)
    rows, wide, dim = attn_in.shape[0], attn_in.shape[1], conv_proj.shape[1]
    high, thin, broad = conv_proj.shape[0], attn_out.shape[0], audio_proj.shape[1]
    lanes = broad - wide
    head = 2 * rows - high
    spare = attn_out[head:].reshape(thin - head, -1, lanes).swapaxes(0, 1).reshape(rows, lanes)
    packed = jnp.concatenate(
        [
            jnp.concatenate([conv_proj, attn_out[:head]]),
            jnp.concatenate([jnp.concatenate([attn_in, spare], 1), audio_proj]),
        ],
        1,
    )
    late_full = lax.all_gather(packed, "seq", axis=0)
    audio_full = late_full[:, rows : 2 * rows, dim:].reshape(-1, broad)
    spare = late_full[:, :rows, dim + wide :].reshape(devices, -1, thin - head, lanes)
    spare = spare.swapaxes(1, 2).reshape(devices, thin - head, dim)
    out_full = jnp.concatenate([late_full[:, high : high + head, :dim], spare], 1).reshape(-1, dim)
    conv_pieces = spread(conv_weight)
    gates = spread_gates(gate_table(expert_ids, gate_weights, experts))
    conv_act = with_pieces(
        conv_kernel,
        16,
        place,
        [spectral, rim],
        conv_pieces,
        (devices * conv_weight.shape[0], channels),
        rows_of(tokens, bins * channels),
        [pltpu.VMEM((3, (bins + 1) * tokens, 2 * channels), jnp.bfloat16)],
        gates,
    )
    embed, query, key_rows = pl.pallas_call(
        functools.partial(embed_kernel, high),
        out_shape=(rows_of(tokens, dim), rows_of(tokens, width), rows_of(tokens, 2 * width)),
        in_specs=[VMEM, VMEM, HBM],
        out_specs=(VMEM, VMEM, VMEM),
        scratch_shapes=[
            pltpu.VMEM((devices * high, dim), jnp.bfloat16),
            pltpu.VMEM((devices * rows, wide), jnp.bfloat16),
            pltpu.SemaphoreType.DMA((devices,)),
            pltpu.SemaphoreType.DMA((devices,)),
        ],
        compiler_params=room(46),
        cost_estimate=pl.CostEstimate(
            flops=8 * 10**9, bytes_accessed=10**7, transcendentals=0
        ),
    )(conv_act, ln_gain[None], late_full)
    left = shifted(key_rows[-WIN:], "seq", 1)
    right = shifted(key_rows[:WIN], "seq", -1)
    ends = jnp.cumsum(recording_lengths).astype(jnp.int32)
    weighted = (w_gate_up[0] * rms_gain[:, None]).astype(jnp.bfloat16)
    fused = jnp.dot(audio_full, weighted, preferred_element_type=jnp.float32)
    fused = fused.astype(jnp.bfloat16)
    encoded, post = pl.pallas_call(
        functools.partial(attend_kernel, devices * tokens),
        out_shape=(rows_of(tokens, dim), rows_of(tokens, dim)),
        in_specs=[SMEM, SMEM] + [VMEM] * 6,
        out_specs=(VMEM, VMEM),
        scratch_shapes=[pltpu.VMEM((tokens, width), jnp.bfloat16)],
        compiler_params=room(8),
        cost_estimate=pl.CostEstimate(
            flops=4 * 10**9, bytes_accessed=4 * 10**6, transcendentals=0
        ),
    )(ends, (me * tokens)[None].astype(jnp.int32), query, left, key_rows, right, embed, out_full)
    audio_sum = jnp.dot(post, audio_full, preferred_element_type=jnp.float32)
    audio_embed = audio_sum.astype(jnp.bfloat16)
    power = jnp.mean(jnp.square(audio_embed.astype(jnp.float32)), -1, keepdims=True)
    scaled = (post.astype(jnp.float32) * lax.rsqrt(power + 1e-06)).astype(jnp.bfloat16)
    return dense_experts(audio_embed, scaled, gates, fused, w_down[0])


def routed_device(
    spectral,
    recording_lengths,
    expert_ids,
    gate_weights,
    conv_weight,
    conv_proj,
    ln_gain,
    attn_in,
    attn_out,
    audio_proj,
    rms_gain,
    w_gate_up,
    w_down,
):
    devices = lax.axis_size("seq")
    local_tokens = expert_ids.shape[0]
    topk = expert_ids.shape[1]
    experts = devices * w_down.shape[0]
    slots = local_tokens * topk // experts + 1
    width = HEADS * HDIM
    channels = conv_weight.shape[1]
    freq_in = spectral.shape[1] // channels
    freq_out = freq_in // 2
    thinker_width = audio_proj.shape[1]
    proj_full = lax.all_gather(audio_proj, "seq", axis=0, tiled=True)
    frame_rim = shifted(spectral[-1:], "seq", 1)
    extended = jnp.concatenate([frame_rim, spectral], 0).reshape(
        2 * local_tokens + 1, freq_in, channels
    )
    extended = jnp.pad(extended, ((0, 0), (1, 0), (0, 0)))
    tap_list = []
    for across in range(3):
        row_set = extended[across : across + 2 * local_tokens : 2]
        for along in range(3):
            tap_list.append(row_set[:, along : along + freq_in : 2, :])
    patches = jnp.concatenate(tap_list, 2).reshape(local_tokens * freq_out, 9 * channels)
    conv_sum = fold_with(patches, lax.all_gather(conv_weight, "seq", axis=0, tiled=True))
    conv_act = (
        jax.nn.gelu(conv_sum, approximate=False)
        .astype(jnp.bfloat16)
        .reshape(local_tokens, freq_out * channels)
    )
    embed_sum = fold_with(conv_act, lax.all_gather(conv_proj, "seq", axis=0, tiled=True))
    embed = embed_sum.astype(jnp.bfloat16)
    normed = (layer_norm(embed.astype(jnp.float32)) * ln_gain).astype(jnp.bfloat16)
    qkv_sum = fold_with(normed, lax.all_gather(attn_in, "seq", axis=0, tiled=True))
    qkv = qkv_sum.astype(jnp.bfloat16)
    key_rows = padded(qkv[:, width:], (("seq", 0),), WIN)
    ends = jnp.cumsum(recording_lengths)
    first = lax.axis_index("seq") * local_tokens
    query_pos = first + jnp.arange(local_tokens, dtype=jnp.int32)
    key_pos = first - WIN + jnp.arange(local_tokens + 2 * WIN, dtype=jnp.int32)
    context = attend(qkv[:, :width], key_rows, query_pos, key_pos, ends, devices * local_tokens)
    branch_sum = fold_with(context, lax.all_gather(attn_out, "seq", axis=0, tiled=True))
    encoded = (embed.astype(jnp.float32) + branch_sum).astype(jnp.bfloat16)
    post = layer_norm(encoded.astype(jnp.float32)).astype(jnp.bfloat16)
    audio_embed = jnp.dot(post, proj_full, preferred_element_type=jnp.float32).astype(jnp.bfloat16)
    flat_ids = expert_ids.reshape(-1)
    onehot = (flat_ids[:, None] == jnp.arange(experts, dtype=jnp.int32)[None, :]).astype(jnp.int32)
    before = jnp.cumsum(onehot, 0) - onehot
    position = jnp.sum(before * onehot, 1)
    slot_index = flat_ids * slots + position
    owner = jnp.full((experts * slots,), local_tokens * topk, jnp.int32)
    owner = owner.at[slot_index].set(jnp.arange(local_tokens * topk, dtype=jnp.int32))
    owner_rows = owner // topk
    gate_up_local = w_gate_up[0]
    down_local = w_down[0]
    sent_rows = rms_norm(audio_embed, rms_gain)
    padded_rows = jnp.concatenate([sent_rows, jnp.zeros((1, sent_rows.shape[1]), jnp.bfloat16)], 0)
    send_buffer = padded_rows[owner_rows].reshape(experts, slots, sent_rows.shape[1])
    received = lax.all_to_all(send_buffer, "seq", split_axis=0, concat_axis=0, tiled=True)
    rows = received.reshape(-1, received.shape[-1])
    result = expert_ffn(rows, gate_up_local, down_local)
    results = result.reshape(received.shape[0], received.shape[1], thinker_width)
    returned = lax.all_to_all(results, "seq", split_axis=0, concat_axis=0, tiled=True)
    picked = returned.reshape(experts * slots, thinker_width)[slot_index].reshape(
        local_tokens, topk, thinker_width
    )
    expert_sum = jnp.sum(picked * gate_weights[:, :, None], 1)
    return (audio_embed.astype(jnp.float32) + expert_sum).astype(jnp.bfloat16)


def on_device(*arrays):
    devices = lax.axis_size("seq")
    experts, topk = devices * arrays[12].shape[0], arrays[2].shape[1]
    if experts <= 2 * topk and devices % 2 == 0:
        return dense_device(*arrays)
    return routed_device(*arrays)


def solution(mesh):
    placed = (
        P(("groups", "seq"), None),
        P("groups"),
        P(("groups", "seq"), None),
        P(("groups", "seq"), None),
        P("seq", None),
        P("seq", None),
        P(),
        P("seq", None),
        P("seq", None),
        P("seq", None),
        P(),
        P("seq", None, None),
        P("seq", None, None),
    )
    return jax.shard_map(
        on_device, mesh=mesh, in_specs=placed, out_specs=P(("groups", "seq"), None), check_vma=False
    )
```
